32 devices in a mesh: row: 8 (over z, x), col: 4 (over y, core).
Axes of the slice: x: 2, y: 2, z: 4, core: 2. Of those that a mesh axis runs over, the one named last changes fastest.
Arguments:
- iterate: float32 [8, 163840], P(None, ('row', 'col')), may hold values from -6 to 6
- residual: float32 [8, 163840], P(None, ('row', 'col')), may hold values from -6 to 6
- stored_tiles: float32 [8, 4, 640, 64, 64], P('row', 'col'), may hold values from -0.3125 to 0.3125
- block_rows: int32 [8, 4, 640], P('row', 'col'), may hold values from 0 to 319
- block_cols: int32 [8, 4, 640], P('row', 'col'), may hold values from 0 to 639
- live_counts: int32 [8, 4], P('row', 'col'), may hold values from 1 to 640, as said below
Outputs:
- h_iterate: float32 [8, 163840], P(None, ('row', 'col'))
- h_residual: float32 [8, 163840], P(None, ('row', 'col'))
The draws below stay inside these ranges and needn't reach their ends.
Inputs may be any that keep to these rules, and one draw needn't show every extreme that they name: Only the first live_counts slots of a device hold stored tiles; the others are not part of the matrix. Some device fills all 640 slots.
All inputs are finite; a program needn't handle non-finite values.
Results may differ from the reference program's by a relative error of at most 0.0003.
Values sent between devices are 32-bit elements; how exact they have to be, the bound alone decides.
No kernel may reach another device: no remote copies, remote signals or barrier semaphores. Data moves between devices by JAX's collectives and lax.ppermute only.
A program may use at most 192 MiB of HBM per device.

```python
import jax
import jax.numpy as jnp
from jax import lax

ROWS_DEV = 5120
BLK = 64
VEC = 8
SLOTS = 640
NDIM = 163840
N_ROW = 8
N_COL = 4


def draw_live_counts(key, part):
    key = jax.random.fold_in(key, 7)
    key_level, key_jitter, key_pick = jax.random.split(key, 3)
    shape_grid = (N_ROW, N_COL)
    levels = jax.random.randint(key_level, shape_grid, 0, 4)
    top_fill = jnp.maximum(SLOTS // 2 ** levels, 1)
    jitter = jax.random.randint(key_jitter, shape_grid, 0, top_fill // 2 + 1)
    filled = jnp.maximum(top_fill - jitter, 1).reshape(-1)
    chosen = jax.random.randint(key_pick, (), 0, N_ROW * N_COL)
    filled = filled.at[chosen].set(SLOTS)
    return filled.reshape(shape_grid).astype(jnp.int32)


def touch_ends(entries, rng, smallest, largest):
    longest = entries.shape.index(max(entries.shape))
    spots = []
    for shift in (0, 1):
        where = [jax.random.randint(jax.random.fold_in(rng, axis), (), 0, length) for axis, length in enumerate(entries.shape)]
        where[longest] = (where[longest] + shift) % entries.shape[longest]
        spots.append(tuple(where))
    return entries.at[spots[0]].set(smallest).at[spots[1]].set(largest)


def block_levels(rng, shape, cuts, least, largest):
    level = 1.0
    for dim, shards_of in cuts:
        draws = jax.random.uniform(jax.random.fold_in(jax.random.fold_in(rng, 6), dim), (shards_of,), jnp.float32, least / len(cuts), largest / len(cuts))
        level = level * jnp.repeat(jnp.exp(draws), shape[dim] // shards_of).reshape((-1,) + (1,) * (len(shape) - 1 - dim))
    return level


def normal_values(rng, dims, spread, bound, cuts=(), held_as=jnp.bfloat16):
    drawn = spread * jax.random.normal(rng, dims, jnp.float32)
    if cuts:
        drawn = drawn * block_levels(rng, dims, cuts, -0.22, 0.18)
    return jnp.clip(drawn, -bound, bound).astype(held_as)


def setup_inputs(seed: int = 0) -> dict:
    splits = jax.random.split(jax.random.key(seed), 7)
    iterate = normal_values(splits[0], (VEC, NDIM), 1.0, 6.0, ((1, 32),), jnp.float32)
    residual = normal_values(splits[1], (VEC, NDIM), 1.0, 6.0, ((1, 32),), jnp.float32)
    stored_tiles = normal_values(splits[2], (N_ROW, N_COL, SLOTS, BLK, BLK), (6 * BLK) ** -0.5, 0.3125, ((0, 8), (1, 4)), jnp.float32)
    block_rows = touch_ends(jax.random.randint(splits[3], (N_ROW, N_COL, SLOTS), 0, N_COL * ROWS_DEV // BLK), jax.random.fold_in(splits[3], 1), 0, (N_COL * ROWS_DEV // BLK) - 1).astype(jnp.int32)
    block_cols = touch_ends(jax.random.randint(splits[4], (N_ROW, N_COL, SLOTS), 0, N_ROW * ROWS_DEV // BLK), jax.random.fold_in(splits[4], 1), 0, (N_ROW * ROWS_DEV // BLK) - 1).astype(jnp.int32)
    live_counts = draw_live_counts(jax.random.fold_in(splits[6], 71), 0)
    return {"iterate": iterate, "residual": residual, "stored_tiles": stored_tiles, "block_rows": block_rows, "block_cols": block_cols, "live_counts": live_counts}


def tile_products(tile_set, rows_idx, cols_idx, live_mask, near_rows, near_cols, row_total, col_total):
    cols_taken = jnp.take(near_cols, cols_idx, axis=1)
    forward = jnp.einsum("sab,vsb->vsa", tile_set, cols_taken, precision=lax.Precision.HIGHEST)
    forward = forward * live_mask[None, :, None]
    row_total = row_total.at[:, rows_idx, :].add(forward)
    rows_taken = jnp.take(near_rows, rows_idx, axis=1)
    mirrored = jnp.einsum("sab,vsa->vsb", tile_set, rows_taken, precision=lax.Precision.HIGHEST)
    mirrored = mirrored * live_mask[None, :, None]
    col_total = col_total.at[:, cols_idx, :].add(mirrored)
    return row_total, col_total


def reference(iterate, residual, stored_tiles, block_rows, block_cols, live_counts):
    stacked = jnp.concatenate([iterate, residual], axis=0)
    vec_count = stacked.shape[0]
    grid_vec = stacked.reshape(vec_count, N_ROW, N_COL, ROWS_DEV)
    device_count = N_ROW * N_COL

    def device_term(result_grid, inputs):
        tile_set, rows_idx, cols_idx, live_count, dev_index = inputs
        row_pos = dev_index // N_COL
        col_pos = dev_index % N_COL
        near_rows = lax.dynamic_index_in_dim(grid_vec, row_pos, 1, keepdims=False)
        near_rows = near_rows.reshape(vec_count, N_COL * ROWS_DEV // BLK, BLK)
        near_cols = lax.dynamic_index_in_dim(grid_vec, col_pos, 2, keepdims=False)
        near_cols = near_cols.reshape(vec_count, N_ROW * ROWS_DEV // BLK, BLK)
        live_mask = (jnp.arange(SLOTS, dtype=jnp.int32) < live_count).astype(jnp.float32)
        row_zero = jnp.zeros(near_rows.shape, jnp.float32)
        col_zero = jnp.zeros(near_cols.shape, jnp.float32)
        row_part, col_part = tile_products(tile_set, rows_idx, cols_idx, live_mask, near_rows, near_cols, row_zero, col_zero)
        result_grid = result_grid.at[:, row_pos].add(row_part.reshape(vec_count, N_COL, ROWS_DEV))
        result_grid = result_grid.at[:, :, col_pos].add(col_part.reshape(vec_count, N_ROW, ROWS_DEV))
        return result_grid, None

    inputs = (
        stored_tiles.reshape(device_count, SLOTS, BLK, BLK),
        block_rows.reshape(device_count, SLOTS),
        block_cols.reshape(device_count, SLOTS),
        live_counts.reshape(device_count),
        jnp.arange(device_count, dtype=jnp.int32),
    )
    start_grid = jnp.zeros((vec_count, N_ROW, N_COL, ROWS_DEV), jnp.float32)
    result_grid, unused = lax.scan(device_term, start_grid, inputs)
    final = result_grid.reshape(vec_count, NDIM)
    return final[:VEC], final[VEC:]
```

```python
import functools

import jax
import jax.numpy as jnp
from jax import lax
from jax.experimental import pallas as pl
from jax.experimental.pallas import tpu as pltpu
from jax.sharding import PartitionSpec as P

BLK = 64
SUB = 8
LANES = 128
VMEM = pl.BlockSpec(memory_space=pltpu.VMEM)
SMEM = pl.BlockSpec(memory_space=pltpu.SMEM)


def ring_order(count):
    half = count // 2
    return [2 * k for k in range(half)] + [2 * k + 1 for k in reversed(range(half))]


def prep_kernel(nrow, ncol, blocks, place, live, it, res, rows, cols, xb, grows, gcols, srows, scols):
    lane = lax.broadcasted_iota(jnp.int32, (SUB, LANES), 1)
    for k in range(blocks // 2):
        a = it[:, k * LANES:(k + 1) * LANES]
        b = res[:, k * LANES:(k + 1) * LANES]
        xb[2 * k * SUB:(2 * k + 1) * SUB, :] = jnp.where(lane < BLK, a, pltpu.roll(b, BLK, 1))
        xb[(2 * k + 1) * SUB:(2 * k + 2) * SUB, :] = jnp.where(lane < BLK, pltpu.roll(a, BLK, 1), b)
    slots = rows.shape[-1]
    alive = lax.broadcasted_iota(jnp.int32, (1, slots), 1) < live[0, 0]

    def split(idx, count):
        chunk = jnp.zeros_like(idx)
        for j in range(1, count):
            chunk += (idx >= j * blocks).astype(jnp.int32)
        return chunk, idx - chunk * blocks

    me = place[0]
    chunk, rest = split(cols[...], nrow)
    pos = jnp.where(chunk % 2 == 0, chunk // 2, nrow - 1 - chunk // 2)
    gap = pos - me
    rel = jnp.where(gap < 0, gap + nrow, gap)
    idx = rel * blocks + rest
    gcols[...] = jnp.where(alive, idx, 0)
    scols[...] = jnp.where(alive, idx, -1)
    major = ncol // 2
    chunk, rest = split(rows[...], ncol)
    gap = chunk // 2 - place[1]
    rel = jnp.where(gap < 0, gap + major, gap) + major * jnp.where(chunk % 2 == place[2], 0, 1)
    idx = rel * blocks + rest
    grows[...] = jnp.where(alive, idx, 0)
    srows[...] = jnp.where(alive, idx, -1)


def tile_kernel(forward, nsrc, slots, gidx, sidx, tiles, *refs):
    srcs, outs = refs[:nsrc], refs[nsrc:-5]
    xall, xg, xt, yhl, hot = refs[-5:]
    step = pl.program_id(0)
    rows_each = srcs[0].shape[0]
    width = sum(o.shape[0] for o in outs) // SUB

    @pl.when(step == 0)
    def _():
        at = 0
        for src in srcs:
            xall[at:at + src.shape[0], :] = src[...]
            at += src.shape[0]

    def take(j, carry):
        for u in range(8):
            s = j * 8 + u
            c = gidx[0, step * LANES + s]
            xg[pl.ds(pl.multiple_of(s * SUB, SUB), SUB), :] = xall[pl.ds(pl.multiple_of(c * SUB, SUB), SUB), :]
        return carry

    lax.fori_loop(0, LANES // 8, take, 0)
    for i in range(SUB):
        xt[i] = xg[pl.ds(i, LANES, stride=SUB), :].T

    lanes_at = pl.multiple_of(step * 2 * LANES, 2 * LANES)
    ids = lax.broadcasted_iota(jnp.int32, (width, LANES), 0)
    match = (ids == sidx[...]).astype(jnp.float32).astype(jnp.bfloat16)
    hot[:, pl.ds(lanes_at, LANES)] = match
    hot[:, pl.ds(pl.multiple_of(lanes_at + LANES, LANES), LANES)] = match

    group = 4 * SUB

    def products(g, carry):
        h, og = g // 2, g % 2

        def term(k, accs):
            if forward:
                parts = [tiles[pl.ds((og * group + o * SUB) * BLK + k, SUB, stride=BLK), :] for o in range(4)]
                t = jnp.concatenate(parts, axis=0)
            else:
                t = tiles[pl.ds(pl.multiple_of(k * BLK + og * group, group), group), :]
            return tuple(acc + t * xt[i, pl.ds(h * BLK + k, 1), :] for i, acc in enumerate(accs))

        zero = jnp.zeros((group, LANES), jnp.float32)
        accs = lax.fori_loop(0, BLK, term, (zero,) * SUB, unroll=8)
        for i, acc in enumerate(accs):
            hi = acc.astype(jnp.bfloat16)
            lo = (acc - hi.astype(jnp.float32)).astype(jnp.bfloat16)
            at = pl.ds(pl.multiple_of(i * LANES + h * BLK + og * group, group), group)
            yhl[at, pl.ds(lanes_at, LANES)] = hi
            yhl[at, pl.ds(pl.multiple_of(lanes_at + LANES, LANES), LANES)] = lo
        return carry

    lax.fori_loop(0, 4, products, 0)

    @pl.when(step == pl.num_programs(0) - 1)
    def _():
        for i in range(0, SUB, 2):
            y = lax.dot_general(
                hot[...], yhl[i * LANES:(i + 2) * LANES, :], (((1,), (1,)), ((), ())), preferred_element_type=jnp.float32
            )
            at = 0
            for out in outs:
                n = out.shape[0] // SUB
                for u in range(2):
                    out[pl.ds(i + u, n, stride=SUB), :] = y[at:at + n, u * LANES:(u + 1) * LANES]
                at += n


def tile_products(forward, gidx, sidx, tiles, srcs, out_blocks):
    slots = tiles.shape[1]
    nsrc = len(srcs)
    width = sum(out_blocks)
    rows = sum(s.shape[0] for s in srcs)
    return pl.pallas_call(
        functools.partial(tile_kernel, forward, nsrc, slots),
        out_shape=tuple(jax.ShapeDtypeStruct((n * SUB, LANES), jnp.float32) for n in out_blocks),
        grid=(slots // LANES,),
        in_specs=[
            SMEM,
            pl.BlockSpec((1, LANES), lambda s: (0, s)),
            pl.BlockSpec((BLK * BLK, LANES), lambda s: (0, s)),
        ]
        + [VMEM] * nsrc,
        out_specs=tuple([VMEM] * len(out_blocks)),
        scratch_shapes=[
            pltpu.VMEM((rows, LANES), jnp.float32),
            pltpu.VMEM((LANES * SUB, LANES), jnp.float32),
            pltpu.VMEM((SUB, LANES, LANES), jnp.float32),
            pltpu.VMEM((SUB * LANES, 2 * slots), jnp.bfloat16),
            pltpu.VMEM((width, 2 * slots), jnp.bfloat16),
        ],
        compiler_params=pltpu.CompilerParams(vmem_limit_bytes=40 << 20),
        cost_estimate=pl.CostEstimate(flops=2 * slots * BLK * BLK * 16, bytes_accessed=tiles.size * 4, transcendentals=0),
        name="forward_products" if forward else "mirrored_products",
    )(gidx, sidx, tiles, *srcs)


def finish_kernel(blocks, nterm, *refs):
    terms, h_it, h_res = refs[:nterm], refs[nterm], refs[nterm + 1]
    lane = lax.broadcasted_iota(jnp.int32, (SUB, LANES), 1)

    def total(k):
        at = slice(k * SUB, (k + 1) * SUB)
        out = terms[0][at, :]
        for term in terms[1:]:
            out = out + term[at, :]
        return out

    for k in range(blocks // 2):
        a, b = total(2 * k), total(2 * k + 1)
        h_it[:, k * LANES:(k + 1) * LANES] = jnp.where(lane < BLK, a, pltpu.roll(b, BLK, 1))
        h_res[:, k * LANES:(k + 1) * LANES] = jnp.where(lane < BLK, pltpu.roll(a, BLK, 1), b)


def body(nrow, ncol, iterate, residual, stored_tiles, block_rows, block_cols, live_counts):
    slots, blk = stored_tiles.shape[2], stored_tiles.shape[3]
    dev = iterate.shape[1]
    blocks = dev // blk
    rows_each = blocks * SUB
    order = ring_order(nrow)
    major = ncol // 2
    tiles = stored_tiles[0, 0].transpose(1, 2, 0).reshape(blk * blk, slots)

    r, c = lax.axis_index("row"), lax.axis_index("col")
    pos = jnp.where(r % 2 == 0, r // 2, nrow - 1 - r // 2)
    place = jnp.stack([pos, c // 2, c % 2]).astype(jnp.int32)
    idx_shape = jax.ShapeDtypeStruct((1, slots), jnp.int32)
    xb, grows, gcols, srows, scols = pl.pallas_call(
        functools.partial(prep_kernel, nrow, ncol, blocks),
        out_shape=(jax.ShapeDtypeStruct((rows_each, LANES), jnp.float32),) + (idx_shape,) * 4,
        in_specs=[SMEM, SMEM, VMEM, VMEM, VMEM, VMEM],
        out_specs=(VMEM,) * 5,
        name="pack",
    )(place, live_counts, iterate, residual, block_rows[0], block_cols[0])

    cw = [(order[p], order[(p + 1) % nrow]) for p in range(nrow)]
    ccw = [(b, a) for a, b in cw]
    core = [(k, k ^ 1) for k in range(ncol)]
    up = [(2 * m + k, 2 * ((m + 1) % major) + k) for m in range(major) for k in range(2)]

    held = [xb]
    for _ in range(major - 1):
        held.append(lax.ppermute(held[-1], "col", up))
    held = [held[0]] + held[:0:-1]
    near_rows = held + [lax.ppermute(h, "col", core) for h in held]

    near_cols = [None] * nrow
    near_cols[0] = xb
    left = right = xb
    for k in range(1, nrow // 2):
        left = lax.ppermute(left, "row", cw)
        right = lax.ppermute(right, "row", ccw)
        near_cols[nrow - k], near_cols[k] = left, right
    mid = rows_each // 2
    left = lax.ppermute(left[:mid], "row", cw)
    right = lax.ppermute(right[mid:], "row", ccw)
    near_cols[nrow // 2:nrow // 2 + 1] = [left, right]

    col_parts = tile_products(
        False, grows, scols, tiles, near_rows, [blocks] * (nrow // 2) + [blocks // 2] * 2 + [blocks] * (nrow // 2 - 1)
    )
    first, last = col_parts[nrow // 2], col_parts[nrow // 2 + 1]
    col_parts = list(col_parts[:nrow // 2]) + [None] + list(col_parts[nrow // 2 + 2:])
    left = lax.ppermute(first, "row", cw)
    right = lax.ppermute(last, "row", ccw)
    for k in range(nrow // 2 - 1, 0, -1):
        a, b = col_parts[k], col_parts[nrow - k]
        if k == nrow // 2 - 1:
            a = jnp.concatenate([a[:mid] + left, a[mid:]], axis=0)
            b = jnp.concatenate([b[:mid], b[mid:] + right], axis=0)
        else:
            a, b = a + left, b + right
        left = lax.ppermute(a, "row", cw)
        right = lax.ppermute(b, "row", ccw)

    own, other = tile_products(True, gcols, srows, tiles, near_cols, [major * blocks] * 2)
    own = own + lax.ppermute(other, "col", core)
    part = own[(major - 1) * rows_each:] if major > 1 else None
    terms = [col_parts[0], left, right, own[:rows_each]]
    for k in range(major - 1, 0, -1):
        got = lax.ppermute(part, "col", up)
        part = got if k == 1 else own[(k - 1) * rows_each:k * rows_each] + got
    if major > 1:
        terms.append(part)

    out_shape = jax.ShapeDtypeStruct(iterate.shape, jnp.float32)
    return pl.pallas_call(
        functools.partial(finish_kernel, blocks, len(terms)),
        out_shape=(out_shape, out_shape),
        in_specs=[VMEM] * len(terms),
        out_specs=(VMEM, VMEM),
        name="unpack",
    )(*terms)


def solution(mesh):
    in_specs = (
        P(None, ("row", "col")),
        P(None, ("row", "col")),
        P("row", "col", None, None, None),
        P("row", "col", None),
        P("row", "col", None),
        P("row", "col"),
    )
    out_specs = (P(None, ("row", "col")), P(None, ("row", "col")))
    run = functools.partial(body, mesh.shape["row"], mesh.shape["col"])
    return jax.shard_map(run, mesh=mesh, in_specs=in_specs, out_specs=out_specs, check_vma=False)
```

```python
import functools

import jax
import jax.numpy as jnp
from jax import lax
from jax.experimental import pallas as pl
from jax.experimental.pallas import tpu as pltpu
from jax.sharding import PartitionSpec as P

BLK = 64
SUB = 8
LANES = 128
PITCH = 40
PAIR = 32
VMEM = pl.BlockSpec(memory_space=pltpu.VMEM)
SMEM = pl.BlockSpec(memory_space=pltpu.SMEM)


def ring_order(count):
    half = count // 2
    return [2 * k for k in range(half)] + [2 * k + 1 for k in reversed(range(half))]


def prep_kernel(nrow, ncol, blocks, place, live, it, res, rows, cols, xb, grows, gcols, srows, scols):
    lane = lax.broadcasted_iota(jnp.int32, (SUB, LANES), 1)
    for k in range(blocks // 2):
        a = it[:, k * LANES:(k + 1) * LANES]
        b = res[:, k * LANES:(k + 1) * LANES]
        xb[2 * k * SUB:(2 * k + 1) * SUB, :] = jnp.where(lane < BLK, a, pltpu.roll(b, BLK, 1))
        xb[(2 * k + 1) * SUB:(2 * k + 2) * SUB, :] = jnp.where(lane < BLK, pltpu.roll(a, BLK, 1), b)
    slots = rows.shape[-1]
    alive = lax.broadcasted_iota(jnp.int32, (1, slots), 1) < live[0, 0]

    def split(idx, count):
        chunk = jnp.zeros_like(idx)
        for j in range(1, count):
            chunk += (idx >= j * blocks).astype(jnp.int32)
        return chunk, idx - chunk * blocks

    me = place[0]
    chunk, rest = split(cols[...], nrow)
    pos = jnp.where(chunk % 2 == 0, chunk // 2, nrow - 1 - chunk // 2)
    gap = pos - me
    rel = jnp.where(gap < 0, gap + nrow, gap)
    idx = rel * blocks + rest
    gcols[...] = jnp.where(alive, idx, 0)
    scols[...] = jnp.where(alive, idx, nrow * blocks)
    major = ncol // 2
    chunk, rest = split(rows[...], ncol)
    gap = chunk // 2 - place[1]
    rel = jnp.where(gap < 0, gap + major, gap) + major * jnp.where(chunk % 2 == place[2], 0, 1)
    idx = rel * blocks + rest
    grows[...] = jnp.where(alive, idx, 0)
    srows[...] = jnp.where(alive, idx, ncol * blocks)


def first_half(rows):
    return lax.broadcasted_iota(jnp.int32, (rows, LANES), 1) < BLK


def split_kernel(tiles, parts, turned):
    half = BLK // 2

    def turn(j, carry):
        a = tiles[pl.ds(pl.multiple_of(j * BLK, BLK), BLK), :]
        b = tiles[pl.ds(pl.multiple_of((j + half) * BLK, BLK), BLK), :]
        turned[pl.ds(j, LANES, stride=PITCH), :] = jnp.concatenate([a, b], axis=0).T
        return carry

    lax.fori_loop(0, half, turn, 0, unroll=32)
    first = first_half(half)

    def split(s, carry):
        x = turned[pl.ds(pl.multiple_of(s * PITCH, SUB), half), :]
        hi = x.astype(jnp.bfloat16).astype(jnp.float32)
        lo = x - hi
        top = jnp.where(first, hi, pltpu.roll(lo, BLK, 1))
        bottom = jnp.where(first, pltpu.roll(hi, BLK, 1), lo)
        both = jnp.concatenate([top, bottom], axis=0).astype(jnp.bfloat16)
        parts[pl.ds(pl.multiple_of(s * BLK, BLK), BLK), :] = both
        return carry

    lax.fori_loop(0, LANES, split, 0, unroll=32)


def split_tiles(tiles):
    slots = tiles.shape[1]
    return pl.pallas_call(
        split_kernel,
        out_shape=jax.ShapeDtypeStruct((slots * BLK, LANES), jnp.bfloat16),
        grid=(slots // LANES,),
        in_specs=[pl.BlockSpec((BLK * BLK, LANES), lambda s: (0, s))],
        out_specs=pl.BlockSpec((LANES * BLK, LANES), lambda s: (s, 0)),
        scratch_shapes=[pltpu.VMEM((LANES * PITCH, LANES), jnp.float32)],
        compiler_params=pltpu.CompilerParams(vmem_limit_bytes=16 << 20),
        cost_estimate=pl.CostEstimate(flops=0, bytes_accessed=30 << 20, transcendentals=0),
        name="split_tiles",
    )(tiles)


def tile_kernel(forward, nsrc, group, live, gidx, sidx, parts, *refs):
    srcs, outs, pairs, acc = refs[:nsrc], refs[nsrc:-2], refs[-2], refs[-1]
    first8 = first_half(SUB)
    at = 0
    some = 4
    first = first_half(some * SUB)
    for src in srcs:
        n = src.shape[0] // SUB

        def pack(k, carry, src=src, at=at):
            x = src[pl.ds(pl.multiple_of(k * some * SUB, some * SUB), some * SUB), :]
            swapped = pltpu.roll(x, BLK, 1)
            his, los = [], []
            for v in (jnp.where(first, x, swapped), jnp.where(first, swapped, x)):
                hi = v.astype(jnp.bfloat16).astype(jnp.float32)
                his.append(hi.reshape(some, SUB, LANES))
                los.append(jnp.where(first, v - hi, 0.0).reshape(some, SUB, LANES))
            rows = jnp.concatenate(his + los, axis=1).reshape(some * PAIR, LANES)
            to = pl.ds(pl.multiple_of((at + k * some) * PAIR, some * PAIR), some * PAIR)
            pairs[to, :] = rows.astype(jnp.bfloat16)
            return carry

        lax.fori_loop(0, n // some, pack, 0, unroll=n // some)
        at += n
    acc[...] = jnp.zeros_like(acc)

    def step(k, carry):
        for u in range(LANES // group):
            s = k * LANES + u * group
            x = jnp.concatenate(
                [pairs[pl.ds(pl.multiple_of(gidx[0, s + t] * PAIR, PAIR), PAIR), :] for t in range(group)], axis=0
            )
            w = parts[pl.ds(pl.multiple_of(s * BLK, BLK), BLK * group), :]
            if forward:
                y = lax.dot_general(x, w, (((1,), (1,)), ((), ())), preferred_element_type=jnp.float32)
            else:
                y = jnp.dot(x[:, :BLK], w, preferred_element_type=jnp.float32)
            for t in range(group):
                at = slice(t * PAIR, t * PAIR + PAIR)
                z = y[at, t // 2 * LANES:(t // 2 + 1) * LANES] if forward else y[at]
                z = z[:2 * SUB] + z[2 * SUB:]
                if not forward:
                    z = z + pltpu.roll(z, BLK, 1)
                    z = jnp.where(first8, z[:SUB], z[SUB:])
                elif t % 2 == 0:
                    z = jnp.where(first8, z[:SUB], pltpu.roll(z[SUB:], BLK, 1))
                else:
                    z = jnp.where(first8, pltpu.roll(z[:SUB], BLK, 1), z[SUB:])
                to = pl.ds(pl.multiple_of(sidx[0, s + t] * SUB, SUB), SUB)
                acc[to, :] += z
        return carry

    lax.fori_loop(0, (live[0, 0] + LANES - 1) // LANES, step, 0)
    at = 0
    for out in outs:
        n = out.shape[0]
        out[...] = acc[at:at + n, :]
        at += n


def tile_products(forward, live, gidx, sidx, parts, srcs, out_blocks):
    slots = gidx.shape[1]
    return pl.pallas_call(
        functools.partial(tile_kernel, forward, len(srcs), 4 if forward else 1),
        out_shape=tuple(jax.ShapeDtypeStruct((n * SUB, LANES), jnp.float32) for n in out_blocks),
        in_specs=[SMEM] * 3 + [VMEM] * (1 + len(srcs)),
        out_specs=tuple([VMEM] * len(out_blocks)),
        scratch_shapes=[
            pltpu.VMEM((sum(s.shape[0] for s in srcs) * PAIR // SUB, LANES), jnp.bfloat16),
            pltpu.VMEM(((sum(out_blocks) + 1) * SUB, LANES), jnp.float32),
        ],
        compiler_params=pltpu.CompilerParams(vmem_limit_bytes=20 << 20),
        cost_estimate=pl.CostEstimate(flops=0, bytes_accessed=25 << 20, transcendentals=0),
        name="forward_products" if forward else "mirrored_products",
    )(live, gidx, sidx, parts, *srcs)


def finish_kernel(blocks, nterm, *refs):
    terms, h_it, h_res = refs[:nterm], refs[nterm], refs[nterm + 1]
    lane = lax.broadcasted_iota(jnp.int32, (SUB, LANES), 1)

    def total(k):
        at = slice(k * SUB, (k + 1) * SUB)
        out = terms[0][at, :]
        for term in terms[1:]:
            out = out + term[at, :]
        return out

    for k in range(blocks // 2):
        a, b = total(2 * k), total(2 * k + 1)
        h_it[:, k * LANES:(k + 1) * LANES] = jnp.where(lane < BLK, a, pltpu.roll(b, BLK, 1))
        h_res[:, k * LANES:(k + 1) * LANES] = jnp.where(lane < BLK, pltpu.roll(a, BLK, 1), b)


def body(nrow, ncol, iterate, residual, stored_tiles, block_rows, block_cols, live_counts):
    slots, blk = stored_tiles.shape[2], stored_tiles.shape[3]
    dev = iterate.shape[1]
    blocks = dev // blk
    rows_each = blocks * SUB
    order = ring_order(nrow)
    major = ncol // 2
    tiles = stored_tiles[0, 0].transpose(1, 2, 0).reshape(blk * blk, slots)

    r, c = lax.axis_index("row"), lax.axis_index("col")
    pos = jnp.where(r % 2 == 0, r // 2, nrow - 1 - r // 2)
    place = jnp.stack([pos, c // 2, c % 2]).astype(jnp.int32)
    idx_shape = jax.ShapeDtypeStruct((1, slots), jnp.int32)
    xb, grows, gcols, srows, scols = pl.pallas_call(
        functools.partial(prep_kernel, nrow, ncol, blocks),
        out_shape=(jax.ShapeDtypeStruct((rows_each, LANES), jnp.float32),) + (idx_shape,) * 4,
        in_specs=[SMEM, SMEM, VMEM, VMEM, VMEM, VMEM],
        out_specs=(VMEM,) * 5,
        name="pack",
    )(place, live_counts, iterate, residual, block_rows[0], block_cols[0])

    cw = [(order[p], order[(p + 1) % nrow]) for p in range(nrow)]
    ccw = [(b, a) for a, b in cw]
    core = [(k, k ^ 1) for k in range(ncol)]
    up = [(2 * m + k, 2 * ((m + 1) % major) + k) for m in range(major) for k in range(2)]

    held = [xb]
    for _ in range(major - 1):
        held.append(lax.ppermute(held[-1], "col", up))
    held = [held[0]] + held[:0:-1]
    near_rows = held + [lax.ppermute(h, "col", core) for h in held]

    near_cols = [None] * nrow
    near_cols[0] = xb
    left = right = xb
    for k in range(1, nrow // 2):
        left = lax.ppermute(left, "row", cw)
        right = lax.ppermute(right, "row", ccw)
        near_cols[nrow - k], near_cols[k] = left, right
    mid = rows_each // 2
    left = lax.ppermute(left[:mid], "row", cw)
    right = lax.ppermute(right[mid:], "row", ccw)
    near_cols[nrow // 2:nrow // 2 + 1] = [left, right]

    parts = split_tiles(tiles)
    col_parts = tile_products(
        False, live_counts, grows, scols, parts, near_rows, [blocks] * (nrow // 2) + [blocks // 2] * 2 + [blocks] * (nrow // 2 - 1)
    )
    first, last = col_parts[nrow // 2], col_parts[nrow // 2 + 1]
    col_parts = list(col_parts[:nrow // 2]) + [None] + list(col_parts[nrow // 2 + 2:])
    left = lax.ppermute(first, "row", cw)
    right = lax.ppermute(last, "row", ccw)
    for k in range(nrow // 2 - 1, 0, -1):
        a, b = col_parts[k], col_parts[nrow - k]
        if k == nrow // 2 - 1:
            a = jnp.concatenate([a[:mid] + left, a[mid:]], axis=0)
            b = jnp.concatenate([b[:mid], b[mid:] + right], axis=0)
        else:
            a, b = a + left, b + right
        left = lax.ppermute(a, "row", cw)
        right = lax.ppermute(b, "row", ccw)

    own, other = tile_products(True, live_counts, gcols, srows, parts, near_cols, [major * blocks] * 2)
    own = own + lax.ppermute(other, "col", core)
    part = own[(major - 1) * rows_each:] if major > 1 else None
    terms = [col_parts[0], left, right, own[:rows_each]]
    for k in range(major - 1, 0, -1):
        got = lax.ppermute(part, "col", up)
        part = got if k == 1 else own[(k - 1) * rows_each:k * rows_each] + got
    if major > 1:
        terms.append(part)

    out_shape = jax.ShapeDtypeStruct(iterate.shape, jnp.float32)
    return pl.pallas_call(
        functools.partial(finish_kernel, blocks, len(terms)),
        out_shape=(out_shape, out_shape),
        in_specs=[VMEM] * len(terms),
        out_specs=(VMEM, VMEM),
        name="unpack",
    )(*terms)


def solution(mesh):
    in_specs = (
        P(None, ("row", "col")),
        P(None, ("row", "col")),
        P("row", "col", None, None, None),
        P("row", "col", None),
        P("row", "col", None),
        P("row", "col"),
    )
    out_specs = (P(None, ("row", "col")), P(None, ("row", "col")))
    run = functools.partial(body, mesh.shape["row"], mesh.shape["col"])
    return jax.shard_map(run, mesh=mesh, in_specs=in_specs, out_specs=out_specs, check_vma=False)
```

```python
import functools

import jax
import jax.numpy as jnp
from jax import lax
from jax.experimental import pallas as pl
from jax.experimental.pallas import tpu as pltpu
from jax.sharding import PartitionSpec as P

BLK = 64
SUB = 8
LANES = 128
PITCH = 40
PAIR = 32
PIECES = 16
VMEM = pl.BlockSpec(memory_space=pltpu.VMEM)
SMEM = pl.BlockSpec(memory_space=pltpu.SMEM)


def ring_order(count):
    half = count // 2
    return [2 * k for k in range(half)] + [2 * k + 1 for k in reversed(range(half))]


def prep_kernel(nrow, ncol, blocks, place, live, it, res, rows, cols, xb, grows, gcols, srows, scols):
    lane = lax.broadcasted_iota(jnp.int32, (SUB, LANES), 1)
    for k in range(blocks // 2):
        a = it[:, k * LANES:(k + 1) * LANES]
        b = res[:, k * LANES:(k + 1) * LANES]
        xb[2 * k * SUB:(2 * k + 1) * SUB, :] = jnp.where(lane < BLK, a, pltpu.roll(b, BLK, 1))
        xb[(2 * k + 1) * SUB:(2 * k + 2) * SUB, :] = jnp.where(lane < BLK, pltpu.roll(a, BLK, 1), b)
    slots = rows.shape[-1]
    alive = lax.broadcasted_iota(jnp.int32, (1, slots), 1) < live[0, 0]

    def split(idx, count):
        chunk = jnp.zeros_like(idx)
        for j in range(1, count):
            chunk += (idx >= j * blocks).astype(jnp.int32)
        return chunk, idx - chunk * blocks

    me = place[0]
    chunk, rest = split(cols[...], nrow)
    pos = jnp.where(chunk % 2 == 0, chunk // 2, nrow - 1 - chunk // 2)
    gap = pos - me
    rel = jnp.where(gap < 0, gap + nrow, gap)
    idx = rel * blocks + rest
    gcols[...] = jnp.where(alive, idx, 0)
    scols[...] = jnp.where(alive, idx, nrow * blocks)
    major = ncol // 2
    chunk, rest = split(rows[...], ncol)
    gap = chunk // 2 - place[1]
    rel = jnp.where(gap < 0, gap + major, gap) + major * jnp.where(chunk % 2 == place[2], 0, 1)
    idx = rel * blocks + rest
    grows[...] = jnp.where(alive, idx, 0)
    srows[...] = jnp.where(alive, idx, ncol * blocks)


def first_half(rows):
    return lax.broadcasted_iota(jnp.int32, (rows, LANES), 1) < BLK


def turn_kernel(tiles, turned, room, sems):
    half = BLK // 2
    slots = tiles.shape[1]
    piece = BLK * BLK // PIECES
    mine = PIECES // 2

    def load(p):
        at = pl.ds(p * piece, piece)
        return pltpu.make_async_copy(tiles.at[at], room.at[at], sems.at[p])

    for p in range(mine):
        load(p).start()
        load(p + mine).start()
    for p in range(mine):
        load(p).wait()
        load(p + mine).wait()
        for j in range(p * half // mine, (p + 1) * half // mine):
            for k in range(slots // LANES):
                lanes = slice(k * LANES, (k + 1) * LANES)
                a = room[j * BLK:(j + 1) * BLK, lanes]
                b = room[(j + half) * BLK:(j + half + 1) * BLK, lanes]
                turned[pl.ds(k * LANES * PITCH + j, LANES, stride=PITCH), :] = jnp.concatenate([a, b], axis=0).T


def turn_tiles(tiles):
    slots = tiles.shape[1]
    return pl.pallas_call(
        turn_kernel,
        out_shape=pltpu.VMEM((slots * PITCH, LANES), jnp.float32),
        in_specs=[pl.BlockSpec(memory_space=pltpu.HBM)],
        out_specs=VMEM,
        scratch_shapes=[pltpu.VMEM(tiles.shape, jnp.float32), pltpu.SemaphoreType.DMA((PIECES,))],
        compiler_params=pltpu.CompilerParams(vmem_limit_bytes=14 << 20),
        cost_estimate=pl.CostEstimate(flops=0, bytes_accessed=1 << 20, transcendentals=0),
        name="turn_tiles",
    )(pltpu.with_memory_space_constraint(tiles, pltpu.HBM))


def split_kernel(turned, parts):
    half = BLK // 2
    first = first_half(half)

    def split(s, carry):
        x = turned[pl.ds(pl.multiple_of(s * PITCH, SUB), half), :]
        hi = x.astype(jnp.bfloat16).astype(jnp.float32)
        lo = x - hi
        top = jnp.where(first, hi, pltpu.roll(lo, BLK, 1))
        bottom = jnp.where(first, pltpu.roll(hi, BLK, 1), lo)
        both = jnp.concatenate([top, bottom], axis=0).astype(jnp.bfloat16)
        parts[pl.ds(pl.multiple_of(s * BLK, BLK), BLK), :] = both
        return carry

    lax.fori_loop(0, turned.shape[0] // PITCH, split, 0, unroll=32)


def split_tiles(turned):
    slots = turned.shape[0] // PITCH
    return pl.pallas_call(
        split_kernel,
        out_shape=jax.ShapeDtypeStruct((slots * BLK, LANES), jnp.bfloat16),
        in_specs=[VMEM],
        out_specs=VMEM,
        compiler_params=pltpu.CompilerParams(vmem_limit_bytes=4 << 20),
        cost_estimate=pl.CostEstimate(flops=0, bytes_accessed=1 << 20, transcendentals=0),
        name="split_tiles",
    )(turned)


def tile_kernel(forward, nsrc, group, live, gidx, sidx, *refs):
    parts, refs = refs[0], refs[1:]
    srcs, outs, pairs, acc = refs[:nsrc], refs[nsrc:-2], refs[-2], refs[-1]
    first8 = first_half(SUB)
    at = 0
    some = 4
    first = first_half(some * SUB)
    for src in srcs:
        n = src.shape[0] // SUB

        def pack(k, carry, src=src, at=at):
            x = src[pl.ds(pl.multiple_of(k * some * SUB, some * SUB), some * SUB), :]
            swapped = pltpu.roll(x, BLK, 1)
            his, los = [], []
            for v in (jnp.where(first, x, swapped), jnp.where(first, swapped, x)):
                hi = v.astype(jnp.bfloat16).astype(jnp.float32)
                his.append(hi.reshape(some, SUB, LANES))
                los.append(jnp.where(first, v - hi, 0.0).reshape(some, SUB, LANES))
            rows = jnp.concatenate(his + los, axis=1).reshape(some * PAIR, LANES)
            to = pl.ds(pl.multiple_of((at + k * some) * PAIR, some * PAIR), some * PAIR)
            pairs[to, :] = rows.astype(jnp.bfloat16)
            return carry

        lax.fori_loop(0, n // some, pack, 0, unroll=n // some)
        at += n
    acc[...] = jnp.zeros_like(acc)

    def step(k, carry):
        for u in range(LANES // group):
            s = k * LANES + u * group
            x = jnp.concatenate(
                [pairs[pl.ds(pl.multiple_of(gidx[0, s + t] * PAIR, PAIR), PAIR), :] for t in range(group)], axis=0
            )
            w = parts[pl.ds(pl.multiple_of(s * BLK, BLK), BLK * group), :]
            if forward:
                y = lax.dot_general(x, w, (((1,), (1,)), ((), ())), preferred_element_type=jnp.float32)
            else:
                y = jnp.dot(x[:, :BLK], w, preferred_element_type=jnp.float32)
            for t in range(group):
                at = slice(t * PAIR, t * PAIR + PAIR)
                z = y[at, t // 2 * LANES:(t // 2 + 1) * LANES] if forward else y[at]
                z = z[:2 * SUB] + z[2 * SUB:]
                if not forward:
                    z = z + pltpu.roll(z, BLK, 1)
                    z = jnp.where(first8, z[:SUB], z[SUB:])
                elif t % 2 == 0:
                    z = jnp.where(first8, z[:SUB], pltpu.roll(z[SUB:], BLK, 1))
                else:
                    z = jnp.where(first8, pltpu.roll(z[:SUB], BLK, 1), z[SUB:])
                to = pl.ds(pl.multiple_of(sidx[0, s + t] * SUB, SUB), SUB)
                acc[to, :] += z
        return carry

    lax.fori_loop(0, (live[0, 0] + LANES - 1) // LANES, step, 0)
    at = 0
    for out in outs:
        n = out.shape[0]
        out[...] = acc[at:at + n, :]
        at += n


def tile_products(forward, live, gidx, sidx, parts, srcs, out_blocks):
    slots = gidx.shape[1]
    return pl.pallas_call(
        functools.partial(tile_kernel, forward, len(srcs), 4 if forward else 1),
        out_shape=tuple(jax.ShapeDtypeStruct((n * SUB, LANES), jnp.float32) for n in out_blocks),
        in_specs=[SMEM] * 3 + [VMEM] * (1 + len(srcs)),
        out_specs=tuple([VMEM] * len(out_blocks)),
        scratch_shapes=[
            pltpu.VMEM((sum(s.shape[0] for s in srcs) * PAIR // SUB, LANES), jnp.bfloat16),
            pltpu.VMEM(((sum(out_blocks) + 1) * SUB, LANES), jnp.float32),
        ],
        compiler_params=pltpu.CompilerParams(vmem_limit_bytes=20 << 20),
        cost_estimate=pl.CostEstimate(flops=0, bytes_accessed=1 << 20, transcendentals=0),
        name="forward_products" if forward else "mirrored_products",
    )(live, gidx, sidx, parts, *srcs)


def finish_kernel(blocks, nterm, *refs):
    terms, h_it, h_res = refs[:nterm], refs[nterm], refs[nterm + 1]
    lane = lax.broadcasted_iota(jnp.int32, (SUB, LANES), 1)

    def total(k):
        at = slice(k * SUB, (k + 1) * SUB)
        out = terms[0][at, :]
        for term in terms[1:]:
            out = out + term[at, :]
        return out

    for k in range(blocks // 2):
        a, b = total(2 * k), total(2 * k + 1)
        h_it[:, k * LANES:(k + 1) * LANES] = jnp.where(lane < BLK, a, pltpu.roll(b, BLK, 1))
        h_res[:, k * LANES:(k + 1) * LANES] = jnp.where(lane < BLK, pltpu.roll(a, BLK, 1), b)


def body(nrow, ncol, iterate, residual, stored_tiles, block_rows, block_cols, live_counts):
    slots, blk = stored_tiles.shape[2], stored_tiles.shape[3]
    dev = iterate.shape[1]
    blocks = dev // blk
    rows_each = blocks * SUB
    order = ring_order(nrow)
    major = ncol // 2
    tiles = stored_tiles[0, 0].transpose(1, 2, 0).reshape(blk * blk, slots)

    r, c = lax.axis_index("row"), lax.axis_index("col")
    pos = jnp.where(r % 2 == 0, r // 2, nrow - 1 - r // 2)
    place = jnp.stack([pos, c // 2, c % 2]).astype(jnp.int32)
    idx_shape = jax.ShapeDtypeStruct((1, slots), jnp.int32)
    xb, grows, gcols, srows, scols = pl.pallas_call(
        functools.partial(prep_kernel, nrow, ncol, blocks),
        out_shape=(jax.ShapeDtypeStruct((rows_each, LANES), jnp.float32),) + (idx_shape,) * 4,
        in_specs=[SMEM, SMEM, VMEM, VMEM, VMEM, VMEM],
        out_specs=(VMEM,) * 5,
        name="pack",
    )(place, live_counts, iterate, residual, block_rows[0], block_cols[0])

    cw = [(order[p], order[(p + 1) % nrow]) for p in range(nrow)]
    ccw = [(b, a) for a, b in cw]
    core = [(k, k ^ 1) for k in range(ncol)]
    up = [(2 * m + k, 2 * ((m + 1) % major) + k) for m in range(major) for k in range(2)]

    half = nrow // 2
    mid = rows_each // 2
    hold = lax.optimization_barrier

    held = [xb]
    near_core = [lax.ppermute(xb, "col", core)]
    near_cols = [None] * nrow
    near_cols[0] = xb
    left = right = xb
    turned = turn_tiles(tiles)
    parts = None
    col_parts = None
    for k in range(1, half):
        left = lax.ppermute(left, "row", cw)
        right = lax.ppermute(right, "row", ccw)
        if k < major:
            held.append(lax.ppermute(held[-1], "col", up))
        if k == 1:
            left, right, turned = hold((left, right, turned))
        if k < major:
            near_core.append(lax.ppermute(held[-1], "col", core))
        near_cols[nrow - k], near_cols[k] = left, right
        if k == 2:
            parts = split_tiles(turned)
            left, right, parts = hold((left, right, parts))
            near_cols[nrow - k], near_cols[k] = left, right
    for k in range(half, major):
        held.append(lax.ppermute(held[-1], "col", up))
        near_core.append(lax.ppermute(held[-1], "col", core))
    near_rows = [held[0]] + held[:0:-1] + [near_core[0]] + near_core[:0:-1]
    col_parts = tile_products(
        False, live_counts, grows, scols, parts, near_rows,
        [blocks] * half + [blocks // 2] * 2 + [blocks] * (half - 1),
    )
    left, right, col_parts = hold((left, right, col_parts))
    near_cols[half + 1], near_cols[half - 1] = left, right
    near_cols[half:half + 1] = [lax.ppermute(left[:mid], "row", cw), lax.ppermute(right[mid:], "row", ccw)]
    first, last = col_parts[half], col_parts[half + 1]
    col_parts = list(col_parts[:half]) + [None] + list(col_parts[half + 2:])

    left = lax.ppermute(first, "row", cw)
    right = lax.ppermute(last, "row", ccw)
    left, right, near_cols = hold((left, right, near_cols))
    own, other = tile_products(True, live_counts, gcols, srows, parts, near_cols, [major * blocks] * 2)
    for k in range(half - 1, 0, -1):
        a, b = col_parts[k], col_parts[nrow - k]
        if k == half - 1:
            a = jnp.concatenate([a[:mid] + left, a[mid:]], axis=0)
            b = jnp.concatenate([b[:mid], b[mid:] + right], axis=0)
        else:
            a, b = a + left, b + right
        left = lax.ppermute(a, "row", cw)
        right = lax.ppermute(b, "row", ccw)
        if k == half - 1:
            left, right, own, other = hold((left, right, own, other))

    own = own + lax.ppermute(other, "col", core)
    part = own[(major - 1) * rows_each:] if major > 1 else None
    terms = [col_parts[0], left, right, own[:rows_each]]
    for k in range(major - 1, 0, -1):
        got = lax.ppermute(part, "col", up)
        part = got if k == 1 else own[(k - 1) * rows_each:k * rows_each] + got
    if major > 1:
        terms.append(part)

    out_shape = jax.ShapeDtypeStruct(iterate.shape, jnp.float32)
    return pl.pallas_call(
        functools.partial(finish_kernel, blocks, len(terms)),
        out_shape=(out_shape, out_shape),
        in_specs=[VMEM] * len(terms),
        out_specs=(VMEM, VMEM),
        compiler_params=pltpu.CompilerParams(vmem_limit_bytes=4 << 20),
        name="unpack",
    )(*terms)


def solution(mesh):
    in_specs = (
        P(None, ("row", "col")),
        P(None, ("row", "col")),
        P("row", "col", None, None, None),
        P("row", "col", None),
        P("row", "col", None),
        P("row", "col"),
    )
    out_specs = (P(None, ("row", "col")), P(None, ("row", "col")))
    run = functools.partial(body, mesh.shape["row"], mesh.shape["col"])
    return jax.shard_map(run, mesh=mesh, in_specs=in_specs, out_specs=out_specs, check_vma=False)
```

```python
import functools

import jax
import jax.numpy as jnp
from jax import lax
from jax.experimental import pallas as pl
from jax.experimental.pallas import tpu as pltpu
from jax.sharding import PartitionSpec as P

BLK = 64
SUB = 8
LANES = 128
PITCH = 40
PAIR = 32
PIECES = 16
VMEM = pl.BlockSpec(memory_space=pltpu.VMEM)
SMEM = pl.BlockSpec(memory_space=pltpu.SMEM)


def ring_order(count):
    half = count // 2
    return [2 * k for k in range(half)] + [2 * k + 1 for k in reversed(range(half))]


def pack_kernel(blocks, it, res, xb):
    lane = lax.broadcasted_iota(jnp.int32, (SUB, LANES), 1)
    for k in range(blocks // 2):
        a = it[:, k * LANES:(k + 1) * LANES]
        b = res[:, k * LANES:(k + 1) * LANES]
        xb[2 * k * SUB:(2 * k + 1) * SUB, :] = jnp.where(lane < BLK, a, pltpu.roll(b, BLK, 1))
        xb[(2 * k + 1) * SUB:(2 * k + 2) * SUB, :] = jnp.where(lane < BLK, pltpu.roll(a, BLK, 1), b)


def index_kernel(nrow, ncol, blocks, live, rows, cols, grows, gcols, srows, scols):
    slots = rows.shape[-1]
    alive = lax.broadcasted_iota(jnp.int32, (1, slots), 1) < live[0, 0]

    def split(idx, count):
        chunk = jnp.zeros_like(idx)
        for j in range(1, count):
            chunk += (idx >= j * blocks).astype(jnp.int32)
        return chunk, idx - chunk * blocks

    r, c = lax.axis_index("row"), lax.axis_index("col")
    me = jnp.where(r % 2 == 0, r // 2, nrow - 1 - r // 2)
    chunk, rest = split(cols[...], nrow)
    pos = jnp.where(chunk % 2 == 0, chunk // 2, nrow - 1 - chunk // 2)
    gap = pos - me
    rel = jnp.where(gap < 0, gap + nrow, gap)
    idx = rel * blocks + rest
    gcols[...] = jnp.where(alive, idx, 0)
    scols[...] = jnp.where(alive, idx, nrow * blocks)
    major = ncol // 2
    chunk, rest = split(rows[...], ncol)
    gap = chunk // 2 - c // 2
    rel = jnp.where(gap < 0, gap + major, gap) + major * jnp.where(chunk % 2 == c % 2, 0, 1)
    idx = rel * blocks + rest
    grows[...] = jnp.where(alive, idx, 0)
    srows[...] = jnp.where(alive, idx, ncol * blocks)


def first_half(rows):
    return lax.broadcasted_iota(jnp.int32, (rows, LANES), 1) < BLK


def turn_kernel(tiles, turned, room, sems):
    half = BLK // 2
    slots = tiles.shape[1]
    piece = BLK * BLK // PIECES
    mine = PIECES // 2

    def load(p):
        at = pl.ds(p * piece, piece)
        return pltpu.make_async_copy(tiles.at[at], room.at[at], sems.at[p])

    for p in range(mine):
        load(p).start()
        load(p + mine).start()
    for p in range(mine):
        load(p).wait()
        load(p + mine).wait()
        for j in range(p * half // mine, (p + 1) * half // mine):
            for k in range(slots // LANES):
                lanes = slice(k * LANES, (k + 1) * LANES)
                a = room[j * BLK:(j + 1) * BLK, lanes]
                b = room[(j + half) * BLK:(j + half + 1) * BLK, lanes]
                turned[pl.ds(k * LANES * PITCH + j, LANES, stride=PITCH), :] = jnp.concatenate([a, b], axis=0).T


def turn_tiles(tiles):
    slots = tiles.shape[1]
    return pl.pallas_call(
        turn_kernel,
        out_shape=pltpu.VMEM((slots * PITCH, LANES), jnp.float32),
        in_specs=[pl.BlockSpec(memory_space=pltpu.HBM)],
        out_specs=VMEM,
        scratch_shapes=[pltpu.VMEM(tiles.shape, jnp.float32), pltpu.SemaphoreType.DMA((PIECES,))],
        compiler_params=pltpu.CompilerParams(vmem_limit_bytes=14 << 20),
        cost_estimate=pl.CostEstimate(flops=0, bytes_accessed=1 << 20, transcendentals=0),
        name="turn_tiles",
    )(pltpu.with_memory_space_constraint(tiles, pltpu.HBM))


def split_kernel(turned, parts):
    half = BLK // 2
    first = first_half(half)

    def split(s, carry):
        x = turned[pl.ds(pl.multiple_of(s * PITCH, SUB), half), :]
        hi = x.astype(jnp.bfloat16).astype(jnp.float32)
        lo = x - hi
        top = jnp.where(first, hi, pltpu.roll(lo, BLK, 1))
        bottom = jnp.where(first, pltpu.roll(hi, BLK, 1), lo)
        both = jnp.concatenate([top, bottom], axis=0).astype(jnp.bfloat16)
        parts[pl.ds(pl.multiple_of(s * BLK, BLK), BLK), :] = both
        return carry

    lax.fori_loop(0, turned.shape[0] // PITCH, split, 0, unroll=32)


def split_tiles(turned):
    slots = turned.shape[0] // PITCH
    return pl.pallas_call(
        split_kernel,
        out_shape=pltpu.VMEM((slots * BLK, LANES), jnp.bfloat16),
        in_specs=[VMEM],
        out_specs=VMEM,
        compiler_params=pltpu.CompilerParams(vmem_limit_bytes=4 << 20),
        cost_estimate=pl.CostEstimate(flops=0, bytes_accessed=1 << 20, transcendentals=0),
        name="split_tiles",
    )(pltpu.with_memory_space_constraint(turned, pltpu.VMEM))


def tile_kernel(forward, nsrc, group, live, gidx, sidx, *refs):
    parts, refs = refs[0], refs[1:]
    srcs, outs, pairs, acc = refs[:nsrc], refs[nsrc:-2], refs[-2], refs[-1]
    first8 = first_half(SUB)
    at = 0
    some = 4
    first = first_half(some * SUB)
    for src in srcs:
        n = src.shape[0] // SUB

        def pack(k, carry, src=src, at=at):
            x = src[pl.ds(pl.multiple_of(k * some * SUB, some * SUB), some * SUB), :]
            swapped = pltpu.roll(x, BLK, 1)
            his, los = [], []
            for v in (jnp.where(first, x, swapped), jnp.where(first, swapped, x)):
                hi = v.astype(jnp.bfloat16).astype(jnp.float32)
                his.append(hi.reshape(some, SUB, LANES))
                los.append(jnp.where(first, v - hi, 0.0).reshape(some, SUB, LANES))
            rows = jnp.concatenate(his + los, axis=1).reshape(some * PAIR, LANES)
            to = pl.ds(pl.multiple_of((at + k * some) * PAIR, some * PAIR), some * PAIR)
            pairs[to, :] = rows.astype(jnp.bfloat16)
            return carry

        lax.fori_loop(0, n // some, pack, 0, unroll=n // some)
        at += n
    acc[...] = jnp.zeros_like(acc)

    def step(k, carry):
        for u in range(LANES // group):
            s = k * LANES + u * group
            x = jnp.concatenate(
                [pairs[pl.ds(pl.multiple_of(gidx[0, s + t] * PAIR, PAIR), PAIR), :] for t in range(group)], axis=0
            )
            w = parts[pl.ds(pl.multiple_of(s * BLK, BLK), BLK * group), :]
            if forward:
                y = lax.dot_general(x, w, (((1,), (1,)), ((), ())), preferred_element_type=jnp.float32)
            else:
                y = jnp.dot(x[:, :BLK], w, preferred_element_type=jnp.float32)
            for t in range(group):
                at = slice(t * PAIR, t * PAIR + PAIR)
                z = y[at, t // 2 * LANES:(t // 2 + 1) * LANES] if forward else y[at]
                z = z[:2 * SUB] + z[2 * SUB:]
                if not forward:
                    z = z + pltpu.roll(z, BLK, 1)
                    z = jnp.where(first8, z[:SUB], z[SUB:])
                elif t % 2 == 0:
                    z = jnp.where(first8, z[:SUB], pltpu.roll(z[SUB:], BLK, 1))
                else:
                    z = jnp.where(first8, pltpu.roll(z[:SUB], BLK, 1), z[SUB:])
                to = pl.ds(pl.multiple_of(sidx[0, s + t] * SUB, SUB), SUB)
                acc[to, :] += z
        return carry

    lax.fori_loop(0, (live[0, 0] + LANES - 1) // LANES, step, 0)
    at = 0
    for out in outs:
        n = out.shape[0]
        out[...] = acc[at:at + n, :]
        at += n


def tile_products(forward, live, gidx, sidx, parts, srcs, out_blocks):
    slots = gidx.shape[1]
    return pl.pallas_call(
        functools.partial(tile_kernel, forward, len(srcs), 4 if forward else 1),
        out_shape=tuple(jax.ShapeDtypeStruct((n * SUB, LANES), jnp.float32) for n in out_blocks),
        in_specs=[SMEM] * 3 + [VMEM] * (1 + len(srcs)),
        out_specs=tuple([VMEM] * len(out_blocks)),
        scratch_shapes=[
            pltpu.VMEM((sum(s.shape[0] for s in srcs) * PAIR // SUB, LANES), jnp.bfloat16),
            pltpu.VMEM(((sum(out_blocks) + 1) * SUB, LANES), jnp.float32),
        ],
        compiler_params=pltpu.CompilerParams(vmem_limit_bytes=20 << 20),
        cost_estimate=pl.CostEstimate(flops=0, bytes_accessed=1 << 20, transcendentals=0),
        name="forward_products" if forward else "mirrored_products",
    )(live, gidx, sidx, pltpu.with_memory_space_constraint(parts, pltpu.VMEM), *srcs)


def finish_kernel(blocks, nterm, *refs):
    halves, terms, h_it, h_res = (refs[:3], refs[3:6]), refs[6:6 + nterm], refs[6 + nterm], refs[7 + nterm]
    lane = lax.broadcasted_iota(jnp.int32, (SUB, LANES), 1)

    def total(k):
        mid = blocks // 2
        at = slice(k * SUB, (k + 1) * SUB)
        out = terms[0][at, :]
        for term in terms[1:]:
            out = out + term[at, :]
        at = slice(k % mid * SUB, (k % mid + 1) * SUB)
        for term in halves[k // mid]:
            out = out + term[at, :]
        return out

    for k in range(blocks // 2):
        a, b = total(2 * k), total(2 * k + 1)
        h_it[:, k * LANES:(k + 1) * LANES] = jnp.where(lane < BLK, a, pltpu.roll(b, BLK, 1))
        h_res[:, k * LANES:(k + 1) * LANES] = jnp.where(lane < BLK, pltpu.roll(a, BLK, 1), b)


def body(nrow, ncol, iterate, residual, stored_tiles, block_rows, block_cols, live_counts):
    slots, blk = stored_tiles.shape[2], stored_tiles.shape[3]
    dev = iterate.shape[1]
    blocks = dev // blk
    rows_each = blocks * SUB
    order = ring_order(nrow)
    major = ncol // 2
    tiles = stored_tiles[0, 0].transpose(1, 2, 0).reshape(blk * blk, slots)

    far_off = functools.partial(pltpu.with_memory_space_constraint, memory_space=pltpu.HBM)
    xb = pl.pallas_call(
        functools.partial(pack_kernel, blocks),
        out_shape=pltpu.VMEM((rows_each, LANES), jnp.float32),
        in_specs=[VMEM, VMEM],
        out_specs=VMEM,
        compiler_params=pltpu.CompilerParams(vmem_limit_bytes=4 << 20),
        name="pack",
    )(far_off(iterate), far_off(residual))
    grows, gcols, srows, scols = pl.pallas_call(
        functools.partial(index_kernel, nrow, ncol, blocks),
        out_shape=(pltpu.VMEM((1, slots), jnp.int32),) * 4,
        in_specs=[SMEM, VMEM, VMEM],
        out_specs=(VMEM,) * 4,
        compiler_params=pltpu.CompilerParams(vmem_limit_bytes=4 << 20),
        cost_estimate=pl.CostEstimate(flops=0, bytes_accessed=1 << 16, transcendentals=0),
        name="index",
    )(live_counts, far_off(block_rows[0]), far_off(block_cols[0]))

    cw = [(order[p], order[(p + 1) % nrow]) for p in range(nrow)]
    ccw = [(b, a) for a, b in cw]
    core = [(k, k ^ 1) for k in range(ncol)]
    up = [(2 * m + k, 2 * ((m + 1) % major) + k) for m in range(major) for k in range(2)]

    half = nrow // 2
    mid = rows_each // 2
    hold = lax.optimization_barrier

    held = [xb]
    near_core = [lax.ppermute(xb, "col", core)]
    near_cols = [None] * nrow
    near_cols[0] = xb
    left = right = xb
    tiles, grows, gcols, srows, scols = hold((tiles, grows, gcols, srows, scols))
    turned = turn_tiles(tiles)
    parts = None
    col_parts = None
    for k in range(1, half):
        left = lax.ppermute(left, "row", cw)
        right = lax.ppermute(right, "row", ccw)
        if k < major:
            held.append(lax.ppermute(held[-1], "col", up))
        if k == 1:
            left, unused = hold((left, turned))
            right, unused = hold((right, turned))
        if k < major:
            near_core.append(lax.ppermute(held[-1], "col", core))
        near_cols[nrow - k], near_cols[k] = left, right
        if k == 2:
            parts = split_tiles(turned)
            left, parts = hold((left, parts))
            right, parts = hold((right, parts))
            near_cols[nrow - k], near_cols[k] = left, right
    for k in range(half, major):
        held.append(lax.ppermute(held[-1], "col", up))
        near_core.append(lax.ppermute(held[-1], "col", core))
    near_rows = [held[0]] + held[:0:-1] + [near_core[0]] + near_core[:0:-1]
    col_parts = tile_products(False, live_counts, grows, scols, parts, near_rows, [blocks // 2] * (2 * nrow))
    left, right, col_parts = hold((left, right, col_parts))
    near_cols[half + 1], near_cols[half - 1] = left, right
    near_cols[half:half + 1] = [lax.ppermute(left[:mid], "row", cw), lax.ppermute(right[mid:], "row", ccw)]

    def send(pair):
        return lax.ppermute(pair[0], "row", cw), lax.ppermute(pair[1], "row", ccw)

    def mine(k, first):
        return col_parts[2 * k + 1 - first], col_parts[2 * ((nrow - k) % nrow) + first]

    def add(pair, more):
        return pair[0] + more[0], pair[1] + more[1]

    far = send(mine(half, 1))
    near = send(mine(half - 1, 0))
    for k in range(half - 1, 0, -1):
        far = hold(far)
        more = add(far, mine(k, 1))
        far = send(more)
        near, unused = hold((near, more))
        if k > 1:
            near = send(add(near, mine(k - 1, 0)))
        if k == half - 1:
            near_cols = hold((near_cols, more))[0]
            own, other = tile_products(True, live_counts, gcols, srows, parts, near_cols, [major * blocks] * 2)
            far, near, own, other = hold((far, near, own, other))

    own = own + lax.ppermute(other, "col", core)
    part = own[(major - 1) * rows_each:] if major > 1 else None
    halves = [(col_parts[0], far[0], near[1]), (col_parts[1], near[0], far[1])]
    terms = [own[:rows_each]]
    for k in range(major - 1, 0, -1):
        got = lax.ppermute(part, "col", up)
        part = got if k == 1 else own[(k - 1) * rows_each:k * rows_each] + got
    if major > 1:
        terms.append(part)

    out_shape = jax.ShapeDtypeStruct(iterate.shape, jnp.float32)
    return pl.pallas_call(
        functools.partial(finish_kernel, blocks, len(terms)),
        out_shape=(out_shape, out_shape),
        in_specs=[VMEM] * (6 + len(terms)),
        out_specs=(VMEM, VMEM),
        compiler_params=pltpu.CompilerParams(vmem_limit_bytes=4 << 20),
        name="unpack",
    )(*halves[0], *halves[1], *terms)


def solution(mesh):
    in_specs = (
        P(None, ("row", "col")),
        P(None, ("row", "col")),
        P("row", "col", None, None, None),
        P("row", "col", None),
        P("row", "col", None),
        P("row", "col"),
    )
    out_specs = (P(None, ("row", "col")), P(None, ("row", "col")))
    run = functools.partial(body, mesh.shape["row"], mesh.shape["col"])
    return jax.shard_map(run, mesh=mesh, in_specs=in_specs, out_specs=out_specs, check_vma=False)
```

```python
import functools

import jax
import jax.numpy as jnp
from jax import lax
from jax.experimental import pallas as pl
from jax.experimental.pallas import tpu as pltpu
from jax.sharding import PartitionSpec as P

BLK = 64
SUB = 8
LANES = 128
PITCH = 40
PAIR = 32
PIECES = 16
VMEM = pl.BlockSpec(memory_space=pltpu.VMEM)
SMEM = pl.BlockSpec(memory_space=pltpu.SMEM)


def ring_order(count):
    half = count // 2
    return [2 * k for k in range(half)] + [2 * k + 1 for k in reversed(range(half))]


def pack_kernel(blocks, it, res, xb):
    lane = lax.broadcasted_iota(jnp.int32, (SUB, LANES), 1)
    for k in range(blocks // 2):
        a = it[:, k * LANES:(k + 1) * LANES]
        b = res[:, k * LANES:(k + 1) * LANES]
        xb[2 * k * SUB:(2 * k + 1) * SUB, :] = jnp.where(lane < BLK, a, pltpu.roll(b, BLK, 1))
        xb[(2 * k + 1) * SUB:(2 * k + 2) * SUB, :] = jnp.where(lane < BLK, pltpu.roll(a, BLK, 1), b)


def index_kernel(nrow, ncol, blocks, live, rows, cols, grows, gcols, srows, scols):
    slots = rows.shape[-1]
    alive = lax.broadcasted_iota(jnp.int32, (1, slots), 1) < live[0, 0]

    def split(idx, count):
        chunk = jnp.zeros_like(idx)
        for j in range(1, count):
            chunk += (idx >= j * blocks).astype(jnp.int32)
        return chunk, idx - chunk * blocks

    r, c = lax.axis_index("row"), lax.axis_index("col")
    me = jnp.where(r % 2 == 0, r // 2, nrow - 1 - r // 2)
    chunk, rest = split(cols[...], nrow)
    pos = jnp.where(chunk % 2 == 0, chunk // 2, nrow - 1 - chunk // 2)
    gap = pos - me
    rel = jnp.where(gap < 0, gap + nrow, gap)
    idx = rel * blocks + rest
    gcols[...] = jnp.where(alive, idx, 0)
    scols[...] = jnp.where(alive, idx, nrow * blocks)
    major = ncol // 2
    chunk, rest = split(rows[...], ncol)
    gap = chunk // 2 - c // 2
    rel = jnp.where(gap < 0, gap + major, gap) + major * jnp.where(chunk % 2 == c % 2, 0, 1)
    idx = rel * blocks + rest
    grows[...] = jnp.where(alive, idx, 0)
    srows[...] = jnp.where(alive, idx, ncol * blocks)


def first_half(rows):
    return lax.broadcasted_iota(jnp.int32, (rows, LANES), 1) < BLK


def turn_kernel(tiles, turned, room, sems):
    half = BLK // 2
    slots = tiles.shape[1]
    piece = BLK * BLK // PIECES
    mine = PIECES // 2

    def load(p):
        at = pl.ds(p * piece, piece)
        return pltpu.make_async_copy(tiles.at[at], room.at[at], sems.at[p])

    for p in range(mine):
        load(p).start()
        load(p + mine).start()
    for p in range(mine):
        load(p).wait()
        load(p + mine).wait()
        for j in range(p * half // mine, (p + 1) * half // mine):
            for k in range(slots // LANES):
                lanes = slice(k * LANES, (k + 1) * LANES)
                a = room[j * BLK:(j + 1) * BLK, lanes]
                b = room[(j + half) * BLK:(j + half + 1) * BLK, lanes]
                turned[pl.ds(k * LANES * PITCH + j, LANES, stride=PITCH), :] = jnp.concatenate([a, b], axis=0).T


def turn_tiles(tiles):
    slots = tiles.shape[1]
    return pl.pallas_call(
        turn_kernel,
        out_shape=pltpu.VMEM((slots * PITCH, LANES), jnp.float32),
        in_specs=[pl.BlockSpec(memory_space=pltpu.HBM)],
        out_specs=VMEM,
        scratch_shapes=[pltpu.VMEM(tiles.shape, jnp.float32), pltpu.SemaphoreType.DMA((PIECES,))],
        compiler_params=pltpu.CompilerParams(vmem_limit_bytes=14 << 20),
        cost_estimate=pl.CostEstimate(flops=0, bytes_accessed=1 << 20, transcendentals=0),
        name="turn_tiles",
    )(pltpu.with_memory_space_constraint(tiles, pltpu.HBM))


def split_kernel(turned, parts):
    half = BLK // 2
    first = first_half(half)

    def split(s, carry):
        x = turned[pl.ds(pl.multiple_of(s * PITCH, SUB), half), :]
        hi = x.astype(jnp.bfloat16).astype(jnp.float32)
        lo = x - hi
        top = jnp.where(first, hi, pltpu.roll(lo, BLK, 1))
        bottom = jnp.where(first, pltpu.roll(hi, BLK, 1), lo)
        both = jnp.concatenate([top, bottom], axis=0).astype(jnp.bfloat16)
        parts[pl.ds(pl.multiple_of(s * BLK, BLK), BLK), :] = both
        return carry

    lax.fori_loop(0, turned.shape[0] // PITCH, split, 0, unroll=32)


def split_tiles(turned):
    slots = turned.shape[0] // PITCH
    return pl.pallas_call(
        split_kernel,
        out_shape=pltpu.VMEM((slots * BLK, LANES), jnp.bfloat16),
        in_specs=[VMEM],
        out_specs=VMEM,
        compiler_params=pltpu.CompilerParams(vmem_limit_bytes=4 << 20),
        cost_estimate=pl.CostEstimate(flops=0, bytes_accessed=1 << 20, transcendentals=0),
        name="split_tiles",
    )(pltpu.with_memory_space_constraint(turned, pltpu.VMEM))


def widen(pairs, srcs, places):
    some = 4
    first = first_half(some * SUB)
    for src, at in zip(srcs, places):
        n = src.shape[0] // SUB

        def pack(k, carry, src=src, at=at):
            x = src[pl.ds(pl.multiple_of(k * some * SUB, some * SUB), some * SUB), :]
            swapped = pltpu.roll(x, BLK, 1)
            his, los = [], []
            for v in (jnp.where(first, x, swapped), jnp.where(first, swapped, x)):
                hi = v.astype(jnp.bfloat16).astype(jnp.float32)
                his.append(hi.reshape(some, SUB, LANES))
                los.append(jnp.where(first, v - hi, 0.0).reshape(some, SUB, LANES))
            rows = jnp.concatenate(his + los, axis=1).reshape(some * PAIR, LANES)
            to = pl.ds(pl.multiple_of((at + k * some) * PAIR, some * PAIR), some * PAIR)
            pairs[to, :] = rows.astype(jnp.bfloat16)
            return carry

        lax.fori_loop(0, n // some, pack, 0, unroll=n // some)


def widen_kernel(places, *refs):
    widen(refs[-1], refs[:-1], places)


def widen_blocks(srcs, places, blocks):
    return pl.pallas_call(
        functools.partial(widen_kernel, places),
        out_shape=pltpu.VMEM((blocks * PAIR, LANES), jnp.bfloat16),
        in_specs=[VMEM] * len(srcs),
        out_specs=VMEM,
        compiler_params=pltpu.CompilerParams(vmem_limit_bytes=4 << 20),
        cost_estimate=pl.CostEstimate(flops=0, bytes_accessed=1 << 20, transcendentals=0),
        name="widen",
    )(*srcs)


def add_products(forward, group, begin, end, live, gidx, sidx, parts, pairs, acc):
    first8 = first_half(SUB)

    def step(k, carry):
        for u in range(LANES // group):
            s = k * LANES + u * group
            x = jnp.concatenate(
                [pairs[pl.ds(pl.multiple_of(gidx[0, s + t] * PAIR, PAIR), PAIR), :] for t in range(group)], axis=0
            )
            w = parts[pl.ds(pl.multiple_of(s * BLK, BLK), BLK * group), :]
            if forward:
                y = lax.dot_general(x, w, (((1,), (1,)), ((), ())), preferred_element_type=jnp.float32)
            else:
                y = jnp.dot(x[:, :BLK], w, preferred_element_type=jnp.float32)
            for t in range(group):
                at = slice(t * PAIR, t * PAIR + PAIR)
                z = y[at, t // 2 * LANES:(t // 2 + 1) * LANES] if forward else y[at]
                z = z[:2 * SUB] + z[2 * SUB:]
                if not forward:
                    z = z + pltpu.roll(z, BLK, 1)
                    z = jnp.where(first8, z[:SUB], z[SUB:])
                elif t % 2 == 0:
                    z = jnp.where(first8, z[:SUB], pltpu.roll(z[SUB:], BLK, 1))
                else:
                    z = jnp.where(first8, pltpu.roll(z[:SUB], BLK, 1), z[SUB:])
                to = pl.ds(pl.multiple_of(sidx[0, s + t] * SUB, SUB), SUB)
                acc[to, :] += z
        return carry

    lax.fori_loop(begin, jnp.minimum((live[0, 0] + LANES - 1) // LANES, end), step, 0)


def mirrored_kernel(nsrc, chunks, live, gidx, sidx, parts, *refs):
    srcs, outs, pairs, acc = refs[:nsrc], refs[nsrc:-2], refs[-2], refs[-1]
    places = [sum(s.shape[0] for s in srcs[:k]) // SUB for k in range(nsrc)]
    widen(pairs, srcs, places)
    acc[...] = jnp.zeros_like(acc)
    add_products(False, 1, 0, chunks, live, gidx, sidx, parts, pairs, acc)
    at = 0
    for out in outs:
        n = out.shape[0]
        out[...] = acc[at:at + n, :]
        at += n


def mirrored_products(live, gidx, sidx, parts, srcs, out_blocks):
    slots = gidx.shape[1]
    return pl.pallas_call(
        functools.partial(mirrored_kernel, len(srcs), slots // LANES),
        out_shape=tuple(pltpu.VMEM((n * SUB, LANES), jnp.float32) for n in out_blocks),
        in_specs=[SMEM] * 3 + [VMEM] * (1 + len(srcs)),
        out_specs=(VMEM,) * len(out_blocks),
        scratch_shapes=[
            pltpu.VMEM((sum(s.shape[0] for s in srcs) * PAIR // SUB, LANES), jnp.bfloat16),
            pltpu.VMEM(((sum(out_blocks) + 1) * SUB, LANES), jnp.float32),
        ],
        compiler_params=pltpu.CompilerParams(vmem_limit_bytes=16 << 20),
        cost_estimate=pl.CostEstimate(flops=0, bytes_accessed=1 << 20, transcendentals=0),
        name="mirrored_products",
    )(live, gidx, sidx, pltpu.with_memory_space_constraint(parts, pltpu.VMEM), *srcs)


def forward_kernel(nsrc, places, begin, end, live, gidx, sidx, parts, *refs):
    srcs, acc, pairs = refs[:nsrc], refs[-2], refs[-1]
    widen(pairs, srcs, places)
    if begin == 0:
        acc[...] = jnp.zeros_like(acc)
    add_products(True, 4, begin, end, live, gidx, sidx, parts, pairs, acc)


def forward_products(live, gidx, sidx, parts, srcs, places, out_blocks, begin, end, pairs, acc=()):
    begun = acc + (pairs,)
    at = 4 + len(srcs)
    return pl.pallas_call(
        functools.partial(forward_kernel, len(srcs), places, begin, end),
        out_shape=(
            pltpu.VMEM(((out_blocks + 1) * SUB, LANES), jnp.float32),
            pltpu.VMEM(pairs.shape, jnp.bfloat16),
        ),
        in_specs=[SMEM] * 3 + [VMEM] * (1 + len(srcs) + len(begun)),
        out_specs=(VMEM,) * 2,
        input_output_aliases={at + k: 2 - len(begun) + k for k in range(len(begun))},
        compiler_params=pltpu.CompilerParams(vmem_limit_bytes=8 << 20),
        cost_estimate=pl.CostEstimate(flops=0, bytes_accessed=1 << 20, transcendentals=0),
        name="forward_products",
    )(live, gidx, sidx, pltpu.with_memory_space_constraint(parts, pltpu.VMEM), *srcs, *begun)


def finish_kernel(blocks, nterm, *refs):
    halves, terms, h_it, h_res = (refs[:3], refs[3:6]), refs[6:6 + nterm], refs[6 + nterm], refs[7 + nterm]
    lane = lax.broadcasted_iota(jnp.int32, (SUB, LANES), 1)

    def total(k):
        mid = blocks // 2
        at = slice(k * SUB, (k + 1) * SUB)
        out = terms[0][at, :]
        for term in terms[1:]:
            out = out + term[at, :]
        at = slice(k % mid * SUB, (k % mid + 1) * SUB)
        for term in halves[k // mid]:
            out = out + term[at, :]
        return out

    for k in range(blocks // 2):
        a, b = total(2 * k), total(2 * k + 1)
        h_it[:, k * LANES:(k + 1) * LANES] = jnp.where(lane < BLK, a, pltpu.roll(b, BLK, 1))
        h_res[:, k * LANES:(k + 1) * LANES] = jnp.where(lane < BLK, pltpu.roll(a, BLK, 1), b)


def body(nrow, ncol, iterate, residual, stored_tiles, block_rows, block_cols, live_counts):
    slots, blk = stored_tiles.shape[2], stored_tiles.shape[3]
    dev = iterate.shape[1]
    blocks = dev // blk
    rows_each = blocks * SUB
    order = ring_order(nrow)
    major = ncol // 2
    tiles = stored_tiles[0, 0].transpose(1, 2, 0).reshape(blk * blk, slots)

    far_off = functools.partial(pltpu.with_memory_space_constraint, memory_space=pltpu.HBM)
    xb = pl.pallas_call(
        functools.partial(pack_kernel, blocks),
        out_shape=pltpu.VMEM((rows_each, LANES), jnp.float32),
        in_specs=[VMEM, VMEM],
        out_specs=VMEM,
        compiler_params=pltpu.CompilerParams(vmem_limit_bytes=4 << 20),
        name="pack",
    )(far_off(iterate), far_off(residual))
    grows, gcols, srows, scols = pl.pallas_call(
        functools.partial(index_kernel, nrow, ncol, blocks),
        out_shape=(pltpu.VMEM((1, slots), jnp.int32),) * 4,
        in_specs=[SMEM, VMEM, VMEM],
        out_specs=(VMEM,) * 4,
        compiler_params=pltpu.CompilerParams(vmem_limit_bytes=4 << 20),
        cost_estimate=pl.CostEstimate(flops=0, bytes_accessed=1 << 16, transcendentals=0),
        name="index",
    )(live_counts, far_off(block_rows[0]), far_off(block_cols[0]))

    cw = [(order[p], order[(p + 1) % nrow]) for p in range(nrow)]
    ccw = [(b, a) for a, b in cw]
    core = [(k, k ^ 1) for k in range(ncol)]
    up = [(2 * m + k, 2 * ((m + 1) % major) + k) for m in range(major) for k in range(2)]

    half = nrow // 2
    mid = rows_each // 2
    hold = lax.optimization_barrier

    held = [xb]
    near_core = [lax.ppermute(xb, "col", core)]
    near_cols = [None] * nrow
    near_cols[0] = xb
    left = right = xb
    tiles, grows, gcols, srows, scols = hold((tiles, grows, gcols, srows, scols))
    turned = turn_tiles(tiles)
    parts = None
    col_parts = None
    for k in range(1, half):
        left = lax.ppermute(left, "row", cw)
        right = lax.ppermute(right, "row", ccw)
        if k < major:
            held.append(lax.ppermute(held[-1], "col", up))
        if k == 1:
            left, unused = hold((left, turned))
            right, unused = hold((right, turned))
        if k < major:
            near_core.append(lax.ppermute(held[-1], "col", core))
        near_cols[nrow - k], near_cols[k] = left, right
        if k == 2:
            parts = split_tiles(turned)
            left, parts = hold((left, parts))
            right, parts = hold((right, parts))
            near_cols[nrow - k], near_cols[k] = left, right
    for k in range(half, major):
        held.append(lax.ppermute(held[-1], "col", up))
        near_core.append(lax.ppermute(held[-1], "col", core))
    near_rows = [held[0]] + held[:0:-1] + [near_core[0]] + near_core[:0:-1]
    chunks = slots // LANES
    col_sums = mirrored_products(live_counts, grows, scols, parts, near_rows, [blocks // 2] * (2 * nrow))

    def send(pair):
        return lax.ppermute(pair[0], "row", cw), lax.ppermute(pair[1], "row", ccw)

    def mine(k, first):
        return col_sums[2 * k + 1 - first], col_sums[2 * ((nrow - k) % nrow) + first]

    def add(pair, more):
        return pair[0] + more[0], pair[1] + more[1]

    left, right, col_sums = hold((left, right, col_sums))
    near_cols[half + 1], near_cols[half - 1] = left, right
    ends = lax.ppermute(left[:mid], "row", cw), lax.ppermute(right[mid:], "row", ccw)
    there = [k for k in range(nrow) if k != half]
    pairs = widen_blocks([near_cols[k] for k in there], [k * blocks for k in there], nrow * blocks)
    far = send(mine(half, 1))
    near, unused = hold((mine(half - 1, 0), pairs))
    near = send(near)
    for k in range(half - 1, 0, -1):
        more = add(far, mine(k, 1))
        far = send(more)
        near, unused = hold((near, more))
        if k > 1:
            near = send(add(near, mine(k - 1, 0)))
        if k == half - 1:
            ends, unused = hold((ends, more))
            row_sums, pairs = forward_products(
                live_counts, gcols, srows, parts, ends, [half * blocks, half * blocks + blocks // 2], ncol * blocks, 0,
                chunks, pairs,
            )
            far, near, row_sums = hold((far, near, row_sums))
    own, other = row_sums[:major * rows_each], row_sums[major * rows_each:2 * major * rows_each]
    own = own + lax.ppermute(other, "col", core)
    part = own[(major - 1) * rows_each:] if major > 1 else None
    halves = [(col_sums[0], far[0], near[1]), (col_sums[1], near[0], far[1])]
    terms = [own[:rows_each]]
    for k in range(major - 1, 0, -1):
        got = lax.ppermute(part, "col", up)
        part = got if k == 1 else own[(k - 1) * rows_each:k * rows_each] + got
    if major > 1:
        terms.append(part)

    out_shape = jax.ShapeDtypeStruct(iterate.shape, jnp.float32)
    return pl.pallas_call(
        functools.partial(finish_kernel, blocks, len(terms)),
        out_shape=(out_shape, out_shape),
        in_specs=[VMEM] * (6 + len(terms)),
        out_specs=(VMEM, VMEM),
        compiler_params=pltpu.CompilerParams(vmem_limit_bytes=4 << 20),
        name="unpack",
    )(*halves[0], *halves[1], *terms)


def solution(mesh):
    in_specs = (
        P(None, ("row", "col")),
        P(None, ("row", "col")),
        P("row", "col", None, None, None),
        P("row", "col", None),
        P("row", "col", None),
        P("row", "col"),
    )
    out_specs = (P(None, ("row", "col")), P(None, ("row", "col")))
    run = functools.partial(body, mesh.shape["row"], mesh.shape["col"])
    return jax.shard_map(run, mesh=mesh, in_specs=in_specs, out_specs=out_specs, check_vma=False)
```

```python
import functools

import jax
import jax.numpy as jnp
from jax import lax
from jax.experimental import pallas as pl
from jax.experimental.pallas import tpu as pltpu
from jax.sharding import PartitionSpec as P

BLK = 64
SUB = 8
LANES = 128
PITCH = 40
PAIR = 32
PIECES = 16
VMEM = pl.BlockSpec(memory_space=pltpu.VMEM)
SMEM = pl.BlockSpec(memory_space=pltpu.SMEM)


def ring_order(count):
    half = count // 2
    return [2 * k for k in range(half)] + [2 * k + 1 for k in reversed(range(half))]


def pack_kernel(blocks, it, res, xb):
    lane = lax.broadcasted_iota(jnp.int32, (SUB, LANES), 1)
    for k in range(blocks // 2):
        a = it[:, k * LANES:(k + 1) * LANES]
        b = res[:, k * LANES:(k + 1) * LANES]
        xb[2 * k * SUB:(2 * k + 1) * SUB, :] = jnp.where(lane < BLK, a, pltpu.roll(b, BLK, 1))
        xb[(2 * k + 1) * SUB:(2 * k + 2) * SUB, :] = jnp.where(lane < BLK, pltpu.roll(a, BLK, 1), b)


def index_kernel(nrow, ncol, blocks, live, rows, cols, grows, gcols, srows, scols):
    slots = rows.shape[-1]
    alive = lax.broadcasted_iota(jnp.int32, (1, slots), 1) < live[0, 0]

    def split(idx, count):
        chunk = jnp.zeros_like(idx)
        for j in range(1, count):
            chunk += (idx >= j * blocks).astype(jnp.int32)
        return chunk, idx - chunk * blocks

    r, c = lax.axis_index("row"), lax.axis_index("col")
    me = jnp.where(r % 2 == 0, r // 2, nrow - 1 - r // 2)
    chunk, rest = split(cols[...], nrow)
    pos = jnp.where(chunk % 2 == 0, chunk // 2, nrow - 1 - chunk // 2)
    gap = pos - me
    rel = jnp.where(gap < 0, gap + nrow, gap)
    idx = rel * blocks + rest
    gcols[...] = jnp.where(alive, idx, 0)
    scols[...] = jnp.where(alive, idx, nrow * blocks)
    major = ncol // 2
    chunk, rest = split(rows[...], ncol)
    gap = chunk // 2 - c // 2
    rel = jnp.where(gap < 0, gap + major, gap) + major * jnp.where(chunk % 2 == c % 2, 0, 1)
    idx = rel * blocks + rest
    grows[...] = jnp.where(alive, idx, 0)
    srows[...] = jnp.where(alive, idx, ncol * blocks)


def first_half(rows):
    return lax.broadcasted_iota(jnp.int32, (rows, LANES), 1) < BLK


def turn_kernel(tiles, turned, room, sems):
    half = BLK // 2
    slots = tiles.shape[1]
    piece = BLK * BLK // PIECES
    mine = PIECES // 2

    def load(p):
        at = pl.ds(p * piece, piece)
        return pltpu.make_async_copy(tiles.at[at], room.at[at], sems.at[p])

    for p in range(mine):
        load(p).start()
        load(p + mine).start()
    for p in range(mine):
        load(p).wait()
        load(p + mine).wait()
        for j in range(p * half // mine, (p + 1) * half // mine):
            for k in range(slots // LANES):
                lanes = slice(k * LANES, (k + 1) * LANES)
                a = room[j * BLK:(j + 1) * BLK, lanes]
                b = room[(j + half) * BLK:(j + half + 1) * BLK, lanes]
                turned[pl.ds(k * LANES * PITCH + j, LANES, stride=PITCH), :] = jnp.concatenate([a, b], axis=0).T


def turn_tiles(tiles):
    slots = tiles.shape[1]
    return pl.pallas_call(
        turn_kernel,
        out_shape=pltpu.VMEM((slots * PITCH, LANES), jnp.float32),
        in_specs=[pl.BlockSpec(memory_space=pltpu.HBM)],
        out_specs=VMEM,
        scratch_shapes=[pltpu.VMEM(tiles.shape, jnp.float32), pltpu.SemaphoreType.DMA((PIECES,))],
        compiler_params=pltpu.CompilerParams(vmem_limit_bytes=14 << 20),
        cost_estimate=pl.CostEstimate(flops=0, bytes_accessed=1 << 20, transcendentals=0),
        name="turn_tiles",
    )(pltpu.with_memory_space_constraint(tiles, pltpu.HBM))


def split_kernel(turned, parts):
    half = BLK // 2
    first = first_half(half)

    def split(s, carry):
        x = turned[pl.ds(pl.multiple_of(s * PITCH, SUB), half), :]
        hi = x.astype(jnp.bfloat16).astype(jnp.float32)
        lo = x - hi
        top = jnp.where(first, hi, pltpu.roll(lo, BLK, 1))
        bottom = jnp.where(first, pltpu.roll(hi, BLK, 1), lo)
        both = jnp.concatenate([top, bottom], axis=0).astype(jnp.bfloat16)
        parts[pl.ds(pl.multiple_of(s * BLK, BLK), BLK), :] = both
        return carry

    lax.fori_loop(0, turned.shape[0] // PITCH, split, 0, unroll=turned.shape[0] // PITCH // 4)


def split_tiles(turned):
    slots = turned.shape[0] // PITCH
    return pl.pallas_call(
        split_kernel,
        out_shape=pltpu.VMEM((slots * BLK, LANES), jnp.bfloat16),
        in_specs=[VMEM],
        out_specs=VMEM,
        compiler_params=pltpu.CompilerParams(vmem_limit_bytes=4 << 20),
        cost_estimate=pl.CostEstimate(flops=0, bytes_accessed=1 << 20, transcendentals=0),
        name="split_tiles",
    )(pltpu.with_memory_space_constraint(turned, pltpu.VMEM))


def widen(pairs, srcs, places):
    some = 4
    first = first_half(some * SUB)
    for src, at in zip(srcs, places):
        n = src.shape[0] // SUB

        def pack(k, carry, src=src, at=at):
            x = src[pl.ds(pl.multiple_of(k * some * SUB, some * SUB), some * SUB), :]
            swapped = pltpu.roll(x, BLK, 1)
            his, los = [], []
            for v in (jnp.where(first, x, swapped), jnp.where(first, swapped, x)):
                hi = v.astype(jnp.bfloat16).astype(jnp.float32)
                his.append(hi.reshape(some, SUB, LANES))
                los.append(jnp.where(first, v - hi, 0.0).reshape(some, SUB, LANES))
            rows = jnp.concatenate(his + los, axis=1).reshape(some * PAIR, LANES)
            to = pl.ds(pl.multiple_of((at + k * some) * PAIR, some * PAIR), some * PAIR)
            pairs[to, :] = rows.astype(jnp.bfloat16)
            return carry

        lax.fori_loop(0, n // some, pack, 0, unroll=n // some)


def widen_kernel(places, *refs):
    widen(refs[-1], refs[:-1], places)


def widen_blocks(srcs, places, blocks):
    return pl.pallas_call(
        functools.partial(widen_kernel, places),
        out_shape=pltpu.VMEM((blocks * PAIR, LANES), jnp.bfloat16),
        in_specs=[VMEM] * len(srcs),
        out_specs=VMEM,
        compiler_params=pltpu.CompilerParams(vmem_limit_bytes=4 << 20),
        cost_estimate=pl.CostEstimate(flops=0, bytes_accessed=1 << 20, transcendentals=0),
        name="widen",
    )(*srcs)


def add_products(forward, group, size, live, gidx, sidx, parts, pairs, acc):
    first8 = first_half(SUB)

    def step(k, carry):
        for u in range(size // group):
            s = k * size + u * group
            x = jnp.concatenate(
                [pairs[pl.ds(pl.multiple_of(gidx[0, s + t] * PAIR, PAIR), PAIR), :] for t in range(group)], axis=0
            )
            w = parts[pl.ds(pl.multiple_of(s * BLK, BLK), BLK * group), :]
            if forward:
                y = lax.dot_general(x, w, (((1,), (1,)), ((), ())), preferred_element_type=jnp.float32)
            else:
                y = jnp.dot(x[:, :BLK], w, preferred_element_type=jnp.float32)
            for t in range(group):
                at = slice(t * PAIR, t * PAIR + PAIR)
                z = y[at, t // 2 * LANES:(t // 2 + 1) * LANES] if forward else y[at]
                z = z[:2 * SUB] + z[2 * SUB:]
                if not forward:
                    z = z + pltpu.roll(z, BLK, 1)
                    z = jnp.where(first8, z[:SUB], z[SUB:])
                elif t % 2 == 0:
                    z = jnp.where(first8, z[:SUB], pltpu.roll(z[SUB:], BLK, 1))
                else:
                    z = jnp.where(first8, pltpu.roll(z[:SUB], BLK, 1), z[SUB:])
                to = pl.ds(pl.multiple_of(sidx[0, s + t] * SUB, SUB), SUB)
                acc[to, :] += z
        return carry

    lax.fori_loop(0, (live[0, 0] + size - 1) // size, step, 0)


def mirrored_kernel(nsrc, size, live, gidx, sidx, parts, *refs):
    srcs, outs, pairs, acc = refs[:nsrc], refs[nsrc:-2], refs[-2], refs[-1]
    places = [sum(s.shape[0] for s in srcs[:k]) // SUB for k in range(nsrc)]
    widen(pairs, srcs, places)
    acc[...] = jnp.zeros_like(acc)
    add_products(False, 1, size, live, gidx, sidx, parts, pairs, acc)
    at = 0
    for out in outs:
        n = out.shape[0]
        out[...] = acc[at:at + n, :]
        at += n


def mirrored_products(live, gidx, sidx, parts, srcs, out_blocks):
    slots = gidx.shape[1]
    return pl.pallas_call(
        functools.partial(mirrored_kernel, len(srcs), slots // 2),
        out_shape=tuple(pltpu.VMEM((n * SUB, LANES), jnp.float32) for n in out_blocks),
        in_specs=[SMEM] * 3 + [VMEM] * (1 + len(srcs)),
        out_specs=(VMEM,) * len(out_blocks),
        scratch_shapes=[
            pltpu.VMEM((sum(s.shape[0] for s in srcs) * PAIR // SUB, LANES), jnp.bfloat16),
            pltpu.VMEM(((sum(out_blocks) + 1) * SUB, LANES), jnp.float32),
        ],
        compiler_params=pltpu.CompilerParams(vmem_limit_bytes=16 << 20),
        cost_estimate=pl.CostEstimate(flops=0, bytes_accessed=1 << 20, transcendentals=0),
        name="mirrored_products",
    )(live, gidx, sidx, pltpu.with_memory_space_constraint(parts, pltpu.VMEM), *srcs)


def forward_kernel(nsrc, places, size, live, gidx, sidx, parts, *refs):
    srcs, acc, pairs = refs[:nsrc], refs[-2], refs[-1]
    widen(pairs, srcs, places)
    acc[...] = jnp.zeros_like(acc)
    add_products(True, 4, size, live, gidx, sidx, parts, pairs, acc)


def forward_products(live, gidx, sidx, parts, srcs, places, out_blocks, pairs):
    slots = gidx.shape[1]
    return pl.pallas_call(
        functools.partial(forward_kernel, len(srcs), places, slots // 2),
        out_shape=(
            pltpu.VMEM(((out_blocks + 1) * SUB, LANES), jnp.float32),
            pltpu.VMEM(pairs.shape, jnp.bfloat16),
        ),
        in_specs=[SMEM] * 3 + [VMEM] * (2 + len(srcs)),
        out_specs=(VMEM,) * 2,
        input_output_aliases={4 + len(srcs): 1},
        compiler_params=pltpu.CompilerParams(vmem_limit_bytes=8 << 20),
        cost_estimate=pl.CostEstimate(flops=0, bytes_accessed=1 << 20, transcendentals=0),
        name="forward_products",
    )(live, gidx, sidx, pltpu.with_memory_space_constraint(parts, pltpu.VMEM), *srcs, pairs)


def finish_kernel(blocks, nterm, *refs):
    halves, terms, h_it, h_res = (refs[:3], refs[3:6]), refs[6:6 + nterm], refs[6 + nterm], refs[7 + nterm]
    lane = lax.broadcasted_iota(jnp.int32, (SUB, LANES), 1)

    def total(k):
        mid = blocks // 2
        at = slice(k * SUB, (k + 1) * SUB)
        out = terms[0][at, :]
        for term in terms[1:]:
            out = out + term[at, :]
        at = slice(k % mid * SUB, (k % mid + 1) * SUB)
        for term in halves[k // mid]:
            out = out + term[at, :]
        return out

    for k in range(blocks // 2):
        a, b = total(2 * k), total(2 * k + 1)
        h_it[:, k * LANES:(k + 1) * LANES] = jnp.where(lane < BLK, a, pltpu.roll(b, BLK, 1))
        h_res[:, k * LANES:(k + 1) * LANES] = jnp.where(lane < BLK, pltpu.roll(a, BLK, 1), b)


def body(nrow, ncol, iterate, residual, stored_tiles, block_rows, block_cols, live_counts):
    slots, blk = stored_tiles.shape[2], stored_tiles.shape[3]
    dev = iterate.shape[1]
    blocks = dev // blk
    rows_each = blocks * SUB
    order = ring_order(nrow)
    major = ncol // 2
    tiles = stored_tiles[0, 0].transpose(1, 2, 0).reshape(blk * blk, slots)

    far_off = functools.partial(pltpu.with_memory_space_constraint, memory_space=pltpu.HBM)
    xb = pl.pallas_call(
        functools.partial(pack_kernel, blocks),
        out_shape=pltpu.VMEM((rows_each, LANES), jnp.float32),
        in_specs=[VMEM, VMEM],
        out_specs=VMEM,
        compiler_params=pltpu.CompilerParams(vmem_limit_bytes=4 << 20),
        name="pack",
    )(far_off(iterate), far_off(residual))
    grows, gcols, srows, scols = pl.pallas_call(
        functools.partial(index_kernel, nrow, ncol, blocks),
        out_shape=(pltpu.VMEM((1, slots), jnp.int32),) * 4,
        in_specs=[SMEM, VMEM, VMEM],
        out_specs=(VMEM,) * 4,
        compiler_params=pltpu.CompilerParams(vmem_limit_bytes=4 << 20),
        cost_estimate=pl.CostEstimate(flops=0, bytes_accessed=1 << 16, transcendentals=0),
        name="index",
    )(live_counts, far_off(block_rows[0]), far_off(block_cols[0]))

    cw = [(order[p], order[(p + 1) % nrow]) for p in range(nrow)]
    ccw = [(b, a) for a, b in cw]
    core = [(k, k ^ 1) for k in range(ncol)]
    up = [(2 * m + k, 2 * ((m + 1) % major) + k) for m in range(major) for k in range(2)]

    half = nrow // 2
    mid = rows_each // 2
    hold = lax.optimization_barrier

    held = [xb]
    near_core = [lax.ppermute(xb, "col", core)]
    near_cols = [None] * nrow
    near_cols[0] = xb
    left = right = xb
    tiles, grows, gcols, srows, scols = hold((tiles, grows, gcols, srows, scols))
    turned = turn_tiles(tiles)
    parts = None
    col_parts = None
    for k in range(1, half):
        left = lax.ppermute(left, "row", cw)
        right = lax.ppermute(right, "row", ccw)
        if k < major:
            held.append(lax.ppermute(held[-1], "col", up))
        if k == 1:
            left, unused = hold((left, turned))
            right, unused = hold((right, turned))
        if k < major:
            near_core.append(lax.ppermute(held[-1], "col", core))
        near_cols[nrow - k], near_cols[k] = left, right
        if k == 2:
            parts = split_tiles(turned)
            left, parts = hold((left, parts))
            right, parts = hold((right, parts))
            near_cols[nrow - k], near_cols[k] = left, right
    for k in range(half, major):
        held.append(lax.ppermute(held[-1], "col", up))
        near_core.append(lax.ppermute(held[-1], "col", core))
    near_rows = [held[0]] + held[:0:-1] + [near_core[0]] + near_core[:0:-1]
    col_sums = mirrored_products(live_counts, grows, scols, parts, near_rows, [blocks // 2] * (2 * nrow))

    def send(pair):
        return lax.ppermute(pair[0], "row", cw), lax.ppermute(pair[1], "row", ccw)

    def mine(k, first):
        return col_sums[2 * k + 1 - first], col_sums[2 * ((nrow - k) % nrow) + first]

    def add(pair, more):
        return pair[0] + more[0], pair[1] + more[1]

    left, right, col_sums = hold((left, right, col_sums))
    near_cols[half + 1], near_cols[half - 1] = left, right
    ends = lax.ppermute(left[:mid], "row", cw), lax.ppermute(right[mid:], "row", ccw)
    there = [k for k in range(nrow) if k != half]
    pairs = widen_blocks([near_cols[k] for k in there], [k * blocks for k in there], nrow * blocks)
    far = send(mine(half, 1))
    near, unused = hold((mine(half - 1, 0), pairs))
    near = send(near)
    for k in range(half - 1, 0, -1):
        more = add(far, mine(k, 1))
        far = send(more)
        near, unused = hold((near, more))
        if k > 1:
            near = send(add(near, mine(k - 1, 0)))
        if k == half - 1:
            ends, unused = hold((ends, more))
            row_sums, unused = forward_products(
                live_counts, gcols, srows, parts, ends, [half * blocks, half * blocks + blocks // 2], ncol * blocks, pairs
            )
            far, near, row_sums = hold((far, near, row_sums))
    own, other = row_sums[:major * rows_each], row_sums[major * rows_each:2 * major * rows_each]
    own = own + lax.ppermute(other, "col", core)
    part = own[(major - 1) * rows_each:] if major > 1 else None
    halves = [(col_sums[0], far[0], near[1]), (col_sums[1], near[0], far[1])]
    terms = [own[:rows_each]]
    for k in range(major - 1, 0, -1):
        got = lax.ppermute(part, "col", up)
        part = got if k == 1 else own[(k - 1) * rows_each:k * rows_each] + got
    if major > 1:
        terms.append(part)

    out_shape = jax.ShapeDtypeStruct(iterate.shape, jnp.float32)
    return pl.pallas_call(
        functools.partial(finish_kernel, blocks, len(terms)),
        out_shape=(out_shape, out_shape),
        in_specs=[VMEM] * (6 + len(terms)),
        out_specs=(VMEM, VMEM),
        compiler_params=pltpu.CompilerParams(vmem_limit_bytes=4 << 20),
        name="unpack",
    )(*halves[0], *halves[1], *terms)


def solution(mesh):
    in_specs = (
        P(None, ("row", "col")),
        P(None, ("row", "col")),
        P("row", "col", None, None, None),
        P("row", "col", None),
        P("row", "col", None),
        P("row", "col"),
    )
    out_specs = (P(None, ("row", "col")), P(None, ("row", "col")))
    run = functools.partial(body, mesh.shape["row"], mesh.shape["col"])
    return jax.shard_map(run, mesh=mesh, in_specs=in_specs, out_specs=out_specs, check_vma=False)
```

```python
import functools

import jax
import jax.numpy as jnp
from jax import lax
from jax.experimental import pallas as pl
from jax.experimental.pallas import tpu as pltpu
from jax.sharding import PartitionSpec as P

BLK = 64
SUB = 8
LANES = 128
PITCH = 40
PAIR = 32
PIECES = 16
VMEM = pl.BlockSpec(memory_space=pltpu.VMEM)
SMEM = pl.BlockSpec(memory_space=pltpu.SMEM)


def ring_order(count):
    half = count // 2
    return [2 * k for k in range(half)] + [2 * k + 1 for k in reversed(range(half))]


def pack_kernel(blocks, it, res, xb):
    lane = lax.broadcasted_iota(jnp.int32, (SUB, LANES), 1)
    for k in range(blocks // 2):
        a = it[:, k * LANES:(k + 1) * LANES]
        b = res[:, k * LANES:(k + 1) * LANES]
        xb[2 * k * SUB:(2 * k + 1) * SUB, :] = jnp.where(lane < BLK, a, pltpu.roll(b, BLK, 1))
        xb[(2 * k + 1) * SUB:(2 * k + 2) * SUB, :] = jnp.where(lane < BLK, pltpu.roll(a, BLK, 1), b)


def index_kernel(nrow, ncol, blocks, live, rows, cols, grows, gcols, srows, scols):
    slots = rows.shape[-1]
    alive = lax.broadcasted_iota(jnp.int32, (1, slots), 1) < live[0, 0]

    def split(idx, count):
        chunk = jnp.zeros_like(idx)
        for j in range(1, count):
            chunk += (idx >= j * blocks).astype(jnp.int32)
        return chunk, idx - chunk * blocks

    r, c = lax.axis_index("row"), lax.axis_index("col")
    me = jnp.where(r % 2 == 0, r // 2, nrow - 1 - r // 2)
    chunk, rest = split(cols[...], nrow)
    pos = jnp.where(chunk % 2 == 0, chunk // 2, nrow - 1 - chunk // 2)
    gap = pos - me
    rel = jnp.where(gap < 0, gap + nrow, gap)
    idx = rel * blocks + rest
    gcols[...] = jnp.where(alive, idx, 0)
    scols[...] = jnp.where(alive, idx, nrow * blocks)
    major = ncol // 2
    chunk, rest = split(rows[...], ncol)
    gap = chunk // 2 - c // 2
    rel = jnp.where(gap < 0, gap + major, gap) + major * jnp.where(chunk % 2 == c % 2, 0, 1)
    idx = rel * blocks + rest
    grows[...] = jnp.where(alive, idx, 0)
    srows[...] = jnp.where(alive, idx, ncol * blocks)


def first_half(rows):
    return lax.broadcasted_iota(jnp.int32, (rows, LANES), 1) < BLK


def turn_kernel(tiles, turned, room, sems):
    half = BLK // 2
    slots = tiles.shape[1]
    piece = BLK * BLK // PIECES
    mine = PIECES // 2

    def load(p):
        at = pl.ds(p * piece, piece)
        return pltpu.make_async_copy(tiles.at[at], room.at[at], sems.at[p])

    for p in range(mine):
        load(p).start()
        load(p + mine).start()
    for p in range(mine):
        load(p).wait()
        load(p + mine).wait()
        for j in range(p * half // mine, (p + 1) * half // mine):
            for k in range(slots // LANES):
                lanes = slice(k * LANES, (k + 1) * LANES)
                a = room[j * BLK:(j + 1) * BLK, lanes]
                b = room[(j + half) * BLK:(j + half + 1) * BLK, lanes]
                turned[pl.ds(k * LANES * PITCH + j, LANES, stride=PITCH), :] = jnp.concatenate([a, b], axis=0).T


def turn_tiles(tiles):
    slots = tiles.shape[1]
    return pl.pallas_call(
        turn_kernel,
        out_shape=pltpu.VMEM((slots * PITCH, LANES), jnp.float32),
        in_specs=[pl.BlockSpec(memory_space=pltpu.HBM)],
        out_specs=VMEM,
        scratch_shapes=[pltpu.VMEM(tiles.shape, jnp.float32), pltpu.SemaphoreType.DMA((PIECES,))],
        compiler_params=pltpu.CompilerParams(vmem_limit_bytes=14 << 20),
        cost_estimate=pl.CostEstimate(flops=0, bytes_accessed=1 << 20, transcendentals=0),
        name="turn_tiles",
    )(pltpu.with_memory_space_constraint(tiles, pltpu.HBM))


def split_kernel(turned, parts):
    half = BLK // 2
    first = first_half(half)

    def split(s, carry):
        x = turned[pl.ds(pl.multiple_of(s * PITCH, SUB), half), :]
        hi = x.astype(jnp.bfloat16).astype(jnp.float32)
        lo = x - hi
        top = jnp.where(first, hi, pltpu.roll(lo, BLK, 1))
        bottom = jnp.where(first, pltpu.roll(hi, BLK, 1), lo)
        both = jnp.concatenate([top, bottom], axis=0).astype(jnp.bfloat16)
        parts[pl.ds(pl.multiple_of(s * BLK, BLK), BLK), :] = both
        return carry

    lax.fori_loop(0, turned.shape[0] // PITCH, split, 0, unroll=turned.shape[0] // PITCH // 4)


def split_tiles(turned):
    slots = turned.shape[0] // PITCH
    return pl.pallas_call(
        split_kernel,
        out_shape=pltpu.VMEM((slots * BLK, LANES), jnp.bfloat16),
        in_specs=[VMEM],
        out_specs=VMEM,
        compiler_params=pltpu.CompilerParams(vmem_limit_bytes=4 << 20),
        cost_estimate=pl.CostEstimate(flops=0, bytes_accessed=1 << 20, transcendentals=0),
        name="split_tiles",
    )(pltpu.with_memory_space_constraint(turned, pltpu.VMEM))


def widen(pairs, srcs, places):
    some = 4
    first = first_half(some * SUB)
    for src, at in zip(srcs, places):
        n = src.shape[0] // SUB

        def pack(k, carry, src=src, at=at):
            x = src[pl.ds(pl.multiple_of(k * some * SUB, some * SUB), some * SUB), :]
            swapped = pltpu.roll(x, BLK, 1)
            his, los = [], []
            for v in (jnp.where(first, x, swapped), jnp.where(first, swapped, x)):
                hi = v.astype(jnp.bfloat16).astype(jnp.float32)
                his.append(hi.reshape(some, SUB, LANES))
                los.append(jnp.where(first, v - hi, 0.0).reshape(some, SUB, LANES))
            rows = jnp.concatenate(his + los, axis=1).reshape(some * PAIR, LANES)
            to = pl.ds(pl.multiple_of((at + k * some) * PAIR, some * PAIR), some * PAIR)
            pairs[to, :] = rows.astype(jnp.bfloat16)
            return carry

        lax.fori_loop(0, n // some, pack, 0, unroll=n // some)


def widen_kernel(places, *refs):
    widen(refs[-1], refs[:-1], places)


def widen_blocks(srcs, places, blocks):
    return pl.pallas_call(
        functools.partial(widen_kernel, places),
        out_shape=pltpu.VMEM((blocks * PAIR, LANES), jnp.bfloat16),
        in_specs=[VMEM] * len(srcs),
        out_specs=VMEM,
        compiler_params=pltpu.CompilerParams(vmem_limit_bytes=4 << 20),
        cost_estimate=pl.CostEstimate(flops=0, bytes_accessed=1 << 20, transcendentals=0),
        name="widen",
    )(*srcs)


def add_products(forward, group, size, live, gidx, sidx, parts, pairs, acc):
    first8 = first_half(SUB)

    def step(k, carry):
        for u in range(size // group):
            s = k * size + u * group
            x = jnp.concatenate(
                [pairs[pl.ds(pl.multiple_of(gidx[0, s + t] * PAIR, PAIR), PAIR), :] for t in range(group)], axis=0
            )
            w = parts[pl.ds(pl.multiple_of(s * BLK, BLK), BLK * group), :]
            if forward:
                y = lax.dot_general(x, w, (((1,), (1,)), ((), ())), preferred_element_type=jnp.float32)
            else:
                y = jnp.dot(x[:, :BLK], w, preferred_element_type=jnp.float32)
            for t in range(group):
                at = slice(t * PAIR, t * PAIR + PAIR)
                z = y[at, t // 2 * LANES:(t // 2 + 1) * LANES] if forward else y[at]
                z = z[:2 * SUB] + z[2 * SUB:]
                if not forward:
                    z = z + pltpu.roll(z, BLK, 1)
                    z = jnp.where(first8, z[:SUB], z[SUB:])
                elif t % 2 == 0:
                    z = jnp.where(first8, z[:SUB], pltpu.roll(z[SUB:], BLK, 1))
                else:
                    z = jnp.where(first8, pltpu.roll(z[:SUB], BLK, 1), z[SUB:])
                to = pl.ds(pl.multiple_of(sidx[0, s + t] * SUB, SUB), SUB)
                acc[to, :] += z
        return carry

    lax.fori_loop(0, (live[0, 0] + size - 1) // size, step, 0)


def mirrored_kernel(nsrc, size, live, gidx, sidx, parts, *refs):
    srcs, outs, pairs, acc = refs[:nsrc], refs[nsrc:-2], refs[-2], refs[-1]
    places = [sum(s.shape[0] for s in srcs[:k]) // SUB for k in range(nsrc)]
    widen(pairs, srcs, places)
    acc[...] = jnp.zeros_like(acc)
    add_products(False, 1, size, live, gidx, sidx, parts, pairs, acc)
    at = 0
    for out in outs:
        n = out.shape[0]
        out[...] = acc[at:at + n, :]
        at += n


def mirrored_products(live, gidx, sidx, parts, srcs, out_blocks):
    slots = gidx.shape[1]
    return pl.pallas_call(
        functools.partial(mirrored_kernel, len(srcs), slots // 2),
        out_shape=tuple(pltpu.VMEM((n * SUB, LANES), jnp.float32) for n in out_blocks),
        in_specs=[SMEM] * 3 + [VMEM] * (1 + len(srcs)),
        out_specs=(VMEM,) * len(out_blocks),
        scratch_shapes=[
            pltpu.VMEM((sum(s.shape[0] for s in srcs) * PAIR // SUB, LANES), jnp.bfloat16),
            pltpu.VMEM(((sum(out_blocks) + 1) * SUB, LANES), jnp.float32),
        ],
        compiler_params=pltpu.CompilerParams(vmem_limit_bytes=16 << 20),
        cost_estimate=pl.CostEstimate(flops=0, bytes_accessed=1 << 20, transcendentals=0),
        name="mirrored_products",
    )(live, gidx, sidx, pltpu.with_memory_space_constraint(parts, pltpu.VMEM), *srcs)


def forward_kernel(nsrc, places, size, live, gidx, sidx, parts, *refs):
    srcs, acc, pairs = refs[:nsrc], refs[-2], refs[-1]
    widen(pairs, srcs, places)
    acc[...] = jnp.zeros_like(acc)
    add_products(True, 4, size, live, gidx, sidx, parts, pairs, acc)


def forward_products(live, gidx, sidx, parts, srcs, places, out_blocks, pairs):
    slots = gidx.shape[1]
    return pl.pallas_call(
        functools.partial(forward_kernel, len(srcs), places, slots // 2),
        out_shape=(
            pltpu.VMEM(((out_blocks + 1) * SUB, LANES), jnp.float32),
            pltpu.VMEM(pairs.shape, jnp.bfloat16),
        ),
        in_specs=[SMEM] * 3 + [VMEM] * (2 + len(srcs)),
        out_specs=(VMEM,) * 2,
        input_output_aliases={4 + len(srcs): 1},
        compiler_params=pltpu.CompilerParams(vmem_limit_bytes=8 << 20),
        cost_estimate=pl.CostEstimate(flops=0, bytes_accessed=1 << 20, transcendentals=0),
        name="forward_products",
    )(live, gidx, sidx, pltpu.with_memory_space_constraint(parts, pltpu.VMEM), *srcs, pairs)


def finish_kernel(blocks, nterm, *refs):
    halves, terms, h_it, h_res = (refs[:2], refs[2:4]), refs[4:4 + nterm], refs[4 + nterm], refs[5 + nterm]
    lane = lax.broadcasted_iota(jnp.int32, (SUB, LANES), 1)

    def total(k):
        mid = blocks // 2
        at = slice(k * SUB, (k + 1) * SUB)
        out = terms[0][at, :]
        for term in terms[1:]:
            out = out + term[at, :]
        at = slice(k % mid * SUB, (k % mid + 1) * SUB)
        for term in halves[k // mid]:
            out = out + term[at, :]
        return out

    for k in range(blocks // 2):
        a, b = total(2 * k), total(2 * k + 1)
        h_it[:, k * LANES:(k + 1) * LANES] = jnp.where(lane < BLK, a, pltpu.roll(b, BLK, 1))
        h_res[:, k * LANES:(k + 1) * LANES] = jnp.where(lane < BLK, pltpu.roll(a, BLK, 1), b)


def body(nrow, ncol, iterate, residual, stored_tiles, block_rows, block_cols, live_counts):
    slots, blk = stored_tiles.shape[2], stored_tiles.shape[3]
    dev = iterate.shape[1]
    blocks = dev // blk
    rows_each = blocks * SUB
    order = ring_order(nrow)
    major = ncol // 2
    tiles = stored_tiles[0, 0].transpose(1, 2, 0).reshape(blk * blk, slots)

    far_off = functools.partial(pltpu.with_memory_space_constraint, memory_space=pltpu.HBM)
    xb = pl.pallas_call(
        functools.partial(pack_kernel, blocks),
        out_shape=pltpu.VMEM((rows_each, LANES), jnp.float32),
        in_specs=[VMEM, VMEM],
        out_specs=VMEM,
        compiler_params=pltpu.CompilerParams(vmem_limit_bytes=4 << 20),
        name="pack",
    )(far_off(iterate), far_off(residual))
    grows, gcols, srows, scols = pl.pallas_call(
        functools.partial(index_kernel, nrow, ncol, blocks),
        out_shape=(pltpu.VMEM((1, slots), jnp.int32),) * 4,
        in_specs=[SMEM, VMEM, VMEM],
        out_specs=(VMEM,) * 4,
        compiler_params=pltpu.CompilerParams(vmem_limit_bytes=4 << 20),
        cost_estimate=pl.CostEstimate(flops=0, bytes_accessed=1 << 16, transcendentals=0),
        name="index",
    )(live_counts, far_off(block_rows[0]), far_off(block_cols[0]))

    cw = [(order[p], order[(p + 1) % nrow]) for p in range(nrow)]
    ccw = [(b, a) for a, b in cw]
    core = [(k, k ^ 1) for k in range(ncol)]
    up = [(2 * m + k, 2 * ((m + 1) % major) + k) for m in range(major) for k in range(2)]

    half = nrow // 2
    mid = rows_each // 2
    hold = lax.optimization_barrier

    held = [xb]
    near_core = [lax.ppermute(xb, "col", core)]
    near_cols = [None] * nrow
    near_cols[0] = xb
    left = right = xb
    tiles, grows, gcols, srows, scols = hold((tiles, grows, gcols, srows, scols))
    turned = turn_tiles(tiles)
    parts = None
    col_parts = None
    for k in range(1, half):
        left = lax.ppermute(left, "row", cw)
        right = lax.ppermute(right, "row", ccw)
        if k < major:
            held.append(lax.ppermute(held[-1], "col", up))
        if k == 1:
            left, unused = hold((left, turned))
            right, unused = hold((right, turned))
        if k < major:
            near_core.append(lax.ppermute(held[-1], "col", core))
        near_cols[nrow - k], near_cols[k] = left, right
        if k == 2:
            parts = split_tiles(turned)
            left, parts = hold((left, parts))
            right, parts = hold((right, parts))
            near_cols[nrow - k], near_cols[k] = left, right
    for k in range(half, major):
        held.append(lax.ppermute(held[-1], "col", up))
        near_core.append(lax.ppermute(held[-1], "col", core))
    near_rows = [held[0]] + held[:0:-1] + [near_core[0]] + near_core[:0:-1]
    col_sums = mirrored_products(live_counts, grows, scols, parts, near_rows, [blocks // 2] * (2 * nrow))

    def send(pair):
        return lax.ppermute(pair[0], "row", cw), lax.ppermute(pair[1], "row", ccw)

    def mine(k, first):
        return col_sums[2 * k + 1 - first], col_sums[2 * ((nrow - k) % nrow) + first]

    def add(pair, more):
        return pair[0] + more[0], pair[1] + more[1]

    left, right, col_sums = hold((left, right, col_sums))
    near_cols[half + 1], near_cols[half - 1] = left, right
    ends = lax.ppermute(left[:mid], "row", cw), lax.ppermute(right[mid:], "row", ccw)
    there = [k for k in range(nrow) if k != half]
    pairs = widen_blocks([near_cols[k] for k in there], [k * blocks for k in there], nrow * blocks)
    far = send(mine(half, 1))
    near, unused = hold((mine(half - 1, 0), pairs))
    near = send(near)
    for k in range(half - 1, 0, -1):
        more = add(far, mine(k, 1))
        far = send(more)
        near, unused = hold((near, more))
        if k > 1:
            near = send(add(near, mine(k - 1, 0)))
        if k == half - 1:
            ends, unused = hold((ends, more))
            row_sums, unused = forward_products(
                live_counts, gcols, srows, parts, ends, [half * blocks, half * blocks + blocks // 2], ncol * blocks, pairs
            )
            far, near, row_sums = hold((far, near, row_sums))
    own, other = row_sums[:major * rows_each], row_sums[major * rows_each:2 * major * rows_each]
    own = own + lax.ppermute(other, "col", core)
    part = own[(major - 1) * rows_each:] if major > 1 else None
    far = add(far, (col_sums[0], col_sums[1]))
    near, far = hold((near, far))
    halves = [(far[0], near[1]), (near[0], far[1])]
    terms = [own[:rows_each]]
    for k in range(major - 1, 0, -1):
        got = lax.ppermute(part, "col", up)
        part = got if k == 1 else own[(k - 1) * rows_each:k * rows_each] + got
    if major > 1:
        terms.append(part)

    out_shape = jax.ShapeDtypeStruct(iterate.shape, jnp.float32)
    return pl.pallas_call(
        functools.partial(finish_kernel, blocks, len(terms)),
        out_shape=(out_shape, out_shape),
        in_specs=[VMEM] * (4 + len(terms)),
        out_specs=(VMEM, VMEM),
        compiler_params=pltpu.CompilerParams(vmem_limit_bytes=4 << 20),
        name="unpack",
    )(*halves[0], *halves[1], *terms)


def solution(mesh):
    in_specs = (
        P(None, ("row", "col")),
        P(None, ("row", "col")),
        P("row", "col", None, None, None),
        P("row", "col", None),
        P("row", "col", None),
        P("row", "col"),
    )
    out_specs = (P(None, ("row", "col")), P(None, ("row", "col")))
    run = functools.partial(body, mesh.shape["row"], mesh.shape["col"])
    return jax.shard_map(run, mesh=mesh, in_specs=in_specs, out_specs=out_specs, check_vma=False)
```
